128 devices in a mesh: row: 4 (over x_hi, core), col: 32 (over z, x_lo, y).
Axes of the slice: x: 4 (x_hi: 2, x_lo: 2; x = x_hi * 2 + x_lo), y: 4, z: 4, core: 2. Of those that a mesh axis runs over, the one named last changes fastest.
Arguments:
- tokens: bfloat16 [2, 2048, 1536], P(None, 'col'), may hold values from -6 to 6
- memory: bfloat16 [2, 192, 1536], P(None, None, 'col'), may hold values from -6 to 6
- clip_lengths: int32 [2, 3], replicated, may hold values from 1 to 2046, as said below
- out_grad: bfloat16 [2, 2048, 1536], P(None, 'col'), may hold values from -6 to 6
- norm_gain: bfloat16 [2, 3, 1536], P(None, None, 'col'), may hold values from 0.25 to 1.75
- norm_bias: bfloat16 [2, 3, 1536], P(None, None, 'col'), may hold values from -1.5 to 1.5
- self_in: bfloat16 [2, 3, 1536, 1536], P(None, None, 'col', 'row'), may hold values from -0.15625 to 0.15625
- self_out: bfloat16 [2, 1536, 1536], P(None, 'row', 'col'), may hold values from -1.5 to 1.5
- text_query: bfloat16 [2, 1536, 1536], P(None, 'col', 'row'), may hold values from -0.15625 to 0.15625
- text_kv: bfloat16 [2, 2, 1536, 1536], P(None, None, 'col', 'row'), may hold values from -0.15625 to 0.15625
- text_out: bfloat16 [2, 1536, 1536], P(None, 'row', 'col'), may hold values from -0.75 to 0.75
- mlp_up: bfloat16 [2, 1536, 6144], P(None, 'col', 'row'), may hold values from -0.15625 to 0.15625
- mlp_down: bfloat16 [2, 6144, 1536], P(None, 'row', 'col'), may hold values from -0.078125 to 0.078125
Outputs:
- output: bfloat16 [2, 2048, 1536], P(None, 'col')
- input_grad: float32 [2, 2048, 1536], P(None, 'col')
- memory_grad: float32 [2, 192, 1536], P(None, None, 'col')
- norm_gain_grad: float32 [2, 3, 1536], P(None, None, 'col')
- norm_bias_grad: float32 [2, 2, 1536], P(None, None, 'col')
- ff_norm_bias_grad: float32 [2, 1536], P(None, 'col')
- self_in_grad: float32 [2, 3, 1536, 1536], P(None, None, 'col', 'row')
- self_out_grad: float32 [2, 1536, 1536], P(None, 'row', 'col')
- text_query_grad: float32 [2, 1536, 1536], P(None, 'col', 'row')
- text_kv_grad: float32 [2, 2, 1536, 1536], P(None, None, 'col', 'row')
- text_out_grad: float32 [2, 1536, 1536], P(None, 'row', 'col')
- mlp_up_grad: float32 [2, 1536, 6144], P(None, 'col', 'row')
- mlp_down_grad: float32 [2, 6144, 1536], P(None, 'row', 'col')
The draws below stay inside these ranges and needn't reach their ends.
Inputs may be any that keep to these rules, and one draw needn't show every extreme that they name: `clip_lengths`: row m holds the lengths of the 3 clips of micro-batch m in order and sums to 2048; the first and the last clip are shorter than 64; in one micro-batch both are exactly 1 frame long.
All inputs are finite; a program needn't handle non-finite values.
Results may differ from the reference program's by a relative error of at most 0.023.
Values may be sent and summed in bfloat16 or wider, within the bound.
No kernel may reach another device: no remote copies, remote signals or barrier semaphores. Data moves between devices by JAX's collectives and lax.ppermute only.
A program may use at most 384 MiB of HBM per device.

```python
import math
import jax
import jax.numpy as jnp
from jax import lax

D = 1536
HEADS = 24
FF = 6144
HEAD = 64
LAYERS = 2
MICRO = 2
CLIPS = 3
TEXT = 64
MB_ROWS = 64
MB_TOK = 2048
MEMB = 192


def draw_clip_lengths(key, part):
    key = jax.random.fold_in(key, 7)
    first_key, last_key, pick_key = jax.random.split(key, 3)
    first_clip = jax.random.randint(first_key, (MICRO,), 1, MB_ROWS)
    last_clip = jax.random.randint(last_key, (MICRO,), 1, MB_ROWS)
    chosen = jax.random.randint(pick_key, (), 0, MICRO)
    single = jnp.arange(MICRO, dtype=jnp.int32) == chosen
    first_clip = jnp.where(single, 1, first_clip)
    last_clip = jnp.where(single, 1, last_clip)
    middle_clip = MB_TOK - first_clip - last_clip
    return jnp.stack([first_clip, middle_clip, last_clip], axis=1).astype(jnp.int32)


def block_scale(key, dims, cuts, least, high):
    factor_of, own = 1.0, jax.random.fold_in(key, 6)
    for position, blocks in cuts:
        draws = jnp.exp(jax.random.uniform(jax.random.fold_in(own, position), (blocks,), jnp.float32, least / len(cuts), high / len(cuts)))
        factor_of = factor_of * jnp.repeat(draws, dims[position] // blocks).reshape([-1 if axis == position else 1 for axis in range(len(dims))])
    return factor_of


def normal_values(key, dims, deviation, limit, cuts=(), kind=jnp.bfloat16):
    values = jax.random.normal(key, dims, jnp.float32) * deviation
    if len(cuts) > 0:
        values = block_scale(key, dims, cuts, -0.22, 0.18) * values
    return jnp.clip(values, min=-limit, max=limit).astype(kind)


def setup_inputs(seed: int = 0) -> dict:
    key_of = jax.random.split(jax.random.key(seed), 14)
    return {
        "tokens": normal_values(key_of[0], (MICRO, MB_TOK, D), 1.0, 6.0, ((1, 32),)),
        "memory": normal_values(key_of[1], (MICRO, MEMB, D), 1.0, 6.0, ((2, 32),)),
        "clip_lengths": draw_clip_lengths(jax.random.fold_in(key_of[13], 71), 0),
        "out_grad": normal_values(key_of[3], (MICRO, MB_TOK, D), 1.0, 6.0, ((1, 32),)),
        "norm_gain": jnp.clip(1.0 + 0.15 * jax.random.normal(key_of[4], (LAYERS, 3, D), jnp.float32), 0.25, 1.75).astype(jnp.bfloat16),
        "norm_bias": normal_values(key_of[5], (LAYERS, 3, D), 0.3, 1.5, ((2, 32),)),
        "self_in": normal_values(key_of[6], (LAYERS, 3, D, D), D ** -0.5, 0.15625, ((2, 32), (3, 4))),
        "self_out": normal_values(key_of[7], (LAYERS, D, D), (HEAD // 4) ** -0.5, 1.5, ((1, 4), (2, 32))),
        "text_query": normal_values(key_of[8], (LAYERS, D, D), D ** -0.5, 0.15625, ((1, 32), (2, 4))),
        "text_kv": normal_values(key_of[9], (LAYERS, 2, D, D), D ** -0.5, 0.15625, ((2, 32), (3, 4))),
        "text_out": normal_values(key_of[10], (LAYERS, D, D), HEAD ** -0.5, 0.75, ((1, 4), (2, 32))),
        "mlp_up": normal_values(key_of[11], (LAYERS, D, FF), D ** -0.5, 0.15625, ((1, 32), (2, 4))),
        "mlp_down": normal_values(key_of[12], (LAYERS, FF, D), FF ** -0.5, 0.078125, ((1, 4), (2, 32))),
    }


NEG_FILL = -1e+30
NORM_EPS = 1e-05
FULL_PRECISION = lax.Precision.HIGHEST

@jax.custom_vjp
def low(v):
    return lax.optimization_barrier(v.astype(jnp.bfloat16)).astype(jnp.float32)

@jax.custom_vjp
def low_back(v):
    return v

def low_keep(v):
    return (low(v), None)

def low_pass(kept, grad):
    return (grad,)

def back_keep(v):
    return (v, None)

def back_low(kept, grad):
    return (low(grad),)
low.defvjp(low_keep, low_pass)
low_back.defvjp(back_keep, back_low)

def layer_norm(values, gain_row, shift_row):
    centre = lax.optimization_barrier(jnp.mean(values, axis=-1, keepdims=True))
    centred = values - centre
    spread = lax.optimization_barrier(jnp.mean(centred * centred, axis=-1, keepdims=True))
    return centred * lax.rsqrt(spread + NORM_EPS) * gain_row + shift_row

def clip_index(positions, lengths):
    clip_ends = jnp.cumsum(lengths)
    return lax.optimization_barrier(jnp.sum((positions[:, None] >= clip_ends[None, :-1]).astype(jnp.int32), axis=1))

def attend(queries, key_rows, value_rows, query_clip, key_clip, causal):
    row_count = queries.shape[0]
    block_rows = min(512, row_count)
    blocks = row_count // block_rows
    score_scale = 1.0 / math.sqrt(HEAD)
    key_heads = key_rows.reshape(key_rows.shape[0], HEADS, HEAD)
    value_heads = value_rows.reshape(value_rows.shape[0], HEADS, HEAD)
    key_places = jnp.arange(key_rows.shape[0], dtype=jnp.int32)

    def one_block(pieces):
        query_block, clip_block, first_row = pieces
        raw_scores = jnp.einsum('qhd,khd->hqk', query_block, key_heads, precision=FULL_PRECISION) * score_scale
        scores = low_back(raw_scores)
        allowed = clip_block[:, None] == key_clip[None, :]
        if causal:
            query_places = first_row + jnp.arange(block_rows, dtype=jnp.int32)
            allowed = allowed & (key_places[None, :] <= query_places[:, None])
        masked = jnp.where(allowed[None], scores, NEG_FILL)
        highest = lax.optimization_barrier(jnp.max(masked, axis=-1, keepdims=True))
        log_total = highest + jnp.log(lax.optimization_barrier(jnp.sum(jnp.exp(masked - highest), axis=-1, keepdims=True)))
        weights = low(jnp.exp(masked - log_total))
        mixed_rows = jnp.einsum('hqk,khd->qhd', weights, value_heads, precision=FULL_PRECISION)
        return mixed_rows.reshape(block_rows, HEADS * HEAD)
    starts = jnp.arange(blocks, dtype=jnp.int32) * block_rows
    mixed_rows = lax.map(jax.checkpoint(one_block), (queries.reshape(blocks, block_rows, HEADS, HEAD), query_clip.reshape(blocks, block_rows), starts))
    return mixed_rows.reshape(row_count, HEADS * HEAD)

def decoder_layer(residual, text_rows, frame_clip, text_clip, gains, shifts, self_in, self_out, text_query, text_kv, text_out, mlp_up, mlp_down):
    normed = low(layer_norm(residual, gains[0], shifts[0]))
    projected = [low_back(low(jnp.dot(normed, self_in[member], precision=FULL_PRECISION))) for member in range(3)]
    mixed_rows = low_back(low(attend(projected[0], projected[1], projected[2], frame_clip, frame_clip, True)))
    residual = residual + low_back(jnp.dot(mixed_rows, self_out, precision=FULL_PRECISION))
    normed = low(layer_norm(residual, gains[1], shifts[1]))
    cross_query = low_back(low(jnp.dot(normed, text_query, precision=FULL_PRECISION)))
    text_keys = low_back(low(jnp.dot(text_rows, text_kv[0], precision=FULL_PRECISION)))
    text_values = low_back(low(jnp.dot(text_rows, text_kv[1], precision=FULL_PRECISION)))
    mixed_rows = low_back(low(attend(cross_query, text_keys, text_values, frame_clip, text_clip, False)))
    residual = residual + low_back(jnp.dot(mixed_rows, text_out, precision=FULL_PRECISION))
    normed = low(layer_norm(residual, gains[2], shifts[2]))
    hidden = low_back(jnp.dot(normed, mlp_up, precision=FULL_PRECISION))
    active = low(jax.nn.gelu(hidden, approximate=False))
    return residual + low_back(jnp.dot(active, mlp_down, precision=FULL_PRECISION))

def forward(tokens, memory, clip_lengths, norm_gain, norm_bias, self_in, self_out, text_query, text_kv, text_out, mlp_up, mlp_down):
    positions = jnp.arange(MB_TOK, dtype=jnp.int32)
    text_clip = jnp.arange(CLIPS * TEXT, dtype=jnp.int32) // TEXT

    def one_batch(pieces):
        residual, text_rows, lengths = pieces
        frame_clip = clip_index(positions, lengths)
        for layer_index in range(LAYERS):
            residual = decoder_layer(residual, text_rows, frame_clip, text_clip, norm_gain[layer_index], norm_bias[layer_index], self_in[layer_index], self_out[layer_index], text_query[layer_index], text_kv[layer_index], text_out[layer_index], mlp_up[layer_index], mlp_down[layer_index])
        return residual
    return lax.map(one_batch, (tokens, memory, clip_lengths))

def reference(tokens, memory, clip_lengths, out_grad, norm_gain, norm_bias, self_in, self_out, text_query, text_kv, text_out, mlp_up, mlp_down):
    floats = tuple((operand.astype(jnp.float32) for operand in (tokens, memory, norm_gain, norm_bias, self_in, self_out, text_query, text_kv, text_out, mlp_up, mlp_down)))

    def run_all(*operands):
        return forward(operands[0], operands[1], clip_lengths, operands[2], operands[3], operands[4], operands[5], operands[6], operands[7], operands[8], operands[9], operands[10])
    result, pull_back = jax.vjp(run_all, *floats)
    gradients = pull_back(out_grad.astype(jnp.float32))
    return (result.astype(jnp.bfloat16), gradients[0], gradients[1], gradients[2], gradients[3][:, 0:2], gradients[3][:, 2], gradients[4], gradients[5], gradients[6], gradients[7], gradients[8], gradients[9], gradients[10])
```

```python
import math

import jax
import jax.numpy as jnp
from jax import lax
from jax.sharding import Mesh, PartitionSpec as P

HEAD = 64
HEADS_HERE = 3
WIDE = HEAD * HEADS_HERE
NEG_FILL = -1e30
NORM_EPS = 1e-05
SCALE = 1.0 / math.sqrt(HEAD)
LOW = jnp.bfloat16
FULL = jnp.float32

FINE = ("xh", "core", "zh", "zl", "xl", "y")
FINE_SIZES = (2, 2, 2, 2, 2, 4)
ROW = ("xh", "core")
COL = ("zh", "zl", "xl", "y")
CHIPS = ("xh", "xl")
SPREAD = ("zh", "zl", "y")
KEYED = ("zl", "y")
SWAP = ((0, 1), (1, 0))


def flipped(size, mask):
    return [(i, i ^ mask) for i in range(size)]


def swapped(x, axis):
    return lax.ppermute(x, axis, SWAP)


def rows_of_all(rows):
    chips = [rows] + [lax.ppermute(rows, CHIPS, flipped(4, d)) for d in (1, 2, 3)]
    half = jnp.concatenate(chips, axis=0)
    return jnp.concatenate([half, swapped(half, "core")], axis=0)


def sum_to_rows(partial):
    count = partial.shape[0] // 8
    blocks = partial.reshape(2, 4, count, partial.shape[1])
    both = blocks[0].astype(FULL) + swapped(blocks[1].astype(LOW), "core").astype(FULL)
    low = both.astype(LOW)
    total = both[0]
    for d in (1, 2, 3):
        total = total + lax.ppermute(low[d], CHIPS, flipped(4, d)).astype(FULL)
    return total


def keys_of_all(block):
    parts = [block]
    for d in range(1, 8):
        parts.append(lax.ppermute(block, KEYED, flipped(8, d)))
    return jnp.concatenate(parts, axis=0)


def sum_to_keys(partial):
    blocks = partial.reshape(8, -1, partial.shape[1])
    low = blocks.astype(LOW)
    total = blocks[0].astype(FULL)
    for d in range(1, 8):
        total = total + lax.ppermute(low[d], KEYED, flipped(8, d)).astype(FULL)
    return total


def mm(a, b, dims):
    return lax.dot_general(a, b, (dims, ((), ())), preferred_element_type=FULL)


def nn(a, b):
    return mm(a, b, ((1,), (0,)))


def nt(a, b):
    return mm(a, b, ((1,), (1,)))


def tn(a, b):
    return mm(a, b, ((0,), (0,)))


def unit(values):
    centre = jnp.mean(values, axis=-1, keepdims=True)
    centred = values - centre
    inverse = lax.rsqrt(jnp.mean(centred * centred, axis=-1, keepdims=True) + NORM_EPS)
    return centred * inverse, inverse


def unit_back(upstream, unit_rows, inverse, gain_row):
    scaled = upstream * gain_row
    inner = (
        scaled
        - jnp.mean(scaled, axis=-1, keepdims=True)
        - unit_rows * jnp.mean(scaled * unit_rows, axis=-1, keepdims=True)
    )
    return inner * inverse


def heads_of(x):
    return x.reshape(x.shape[0], HEADS_HERE, HEAD)


def scores_of(q, k, allowed):
    raw = jnp.einsum("qhd,khd->hqk", heads_of(q), heads_of(k), preferred_element_type=FULL) * SCALE
    return jnp.where(allowed[None], raw, NEG_FILL)


def attend(q, k, v, allowed):
    s = scores_of(q, k, allowed)
    top = jnp.max(s, axis=-1, keepdims=True)
    lse = top + jnp.log(jnp.sum(jnp.exp(s - top), axis=-1, keepdims=True))
    p = jnp.exp(s - lse).astype(LOW)
    o = jnp.einsum("hqk,khd->qhd", p, heads_of(v), preferred_element_type=FULL)
    return o.reshape(q.shape).astype(LOW), lse


def attend_back(do, q, k, v, allowed, lse):
    p = jnp.exp(scores_of(q, k, allowed) - lse)
    dp = jnp.einsum("qhd,khd->hqk", heads_of(do), heads_of(v), preferred_element_type=FULL)
    ds = (p * (dp - jnp.sum(p * dp, axis=-1, keepdims=True))).astype(LOW)
    dq = jnp.einsum("hqk,khd->qhd", ds, heads_of(k), preferred_element_type=FULL) * SCALE
    dk = jnp.einsum("hqk,qhd->khd", ds, heads_of(q), preferred_element_type=FULL) * SCALE
    dv = jnp.einsum("hqk,qhd->khd", p.astype(LOW), heads_of(do), preferred_element_type=FULL)
    return dq.reshape(q.shape), dk.reshape(k.shape), dv.reshape(v.shape)


def gelu(z):
    return 0.5 * z * (1.0 + lax.erf(z * math.sqrt(0.5)))


def gelu_slope(z):
    half = 0.5 * (1.0 + lax.erf(z * math.sqrt(0.5)))
    return half + z * jnp.exp(-0.5 * z * z) * (1.0 / math.sqrt(2.0 * math.pi))


def width_mixed(x):
    lead = x.shape[:-1]
    parts = x.reshape(*lead, 4, 2, 4, -1)
    return jnp.swapaxes(parts, -2, -3).reshape(*lead, -1)


def width_restored(x):
    lead = x.shape[:-1]
    parts = x.reshape(*lead, 4, 4, 2, -1)
    return jnp.swapaxes(parts, -2, -3).reshape(*lead, -1)


def local(
    tokens,
    memory,
    clip_lengths,
    out_grad,
    norm_gain,
    norm_bias,
    self_in,
    self_out,
    text_query,
    text_kv,
    text_out,
    mlp_up,
    mlp_down,
):
    xh, core, zh = lax.axis_index("xh"), lax.axis_index("core"), lax.axis_index("zh")
    zl, xl, y = lax.axis_index("zl"), lax.axis_index("xl"), lax.axis_index("y")
    row = xh * 2 + core
    width = tokens.shape[2]
    strip = memory.shape[2]
    ff = mlp_up.shape[2] // 2

    def halves(x, axis):
        size = x.shape[axis] // 2
        a = lax.slice_in_dim(x, 0, size, axis=axis)
        b = lax.slice_in_dim(x, size, 2 * size, axis=axis)
        return a, b

    def joined(*pairs):
        return tuple(jnp.concatenate(side, axis=1) for side in zip(*pairs))

    def common(x):
        return x, x

    def spread(pair):
        first, second = pair
        mine = jnp.where(xl == 0, first, second)
        theirs = swapped(jnp.where(xl == 0, second, first), "xl")
        both = jnp.where(
            xl == 0, jnp.concatenate([mine, theirs]), jnp.concatenate([theirs, mine])
        )
        return lax.all_gather(both, SPREAD, axis=0, tiled=True)

    norms = jnp.concatenate([norm_gain.reshape(6, strip), norm_bias.reshape(6, strip)])
    norms = jnp.pad(norms.T, ((0, 0), (0, 52)))
    memory_t = memory.reshape(-1, strip).T

    def own_in(l):
        return joined(*[halves(self_in[l, k], 1) for k in range(3)])

    def own_out(w, l):
        return halves(w[l].T, 1)

    def own_text(l):
        return joined(*[halves(text_kv[l, k], 1) for k in range(2)])

    def own_ff(l):
        return joined(halves(mlp_up[l], 1), own_out(mlp_down, l))

    piece_0 = spread(joined(own_in(0), common(norms)))
    piece_1 = spread(
        joined(
            own_text(0),
            common(memory_t),
            own_out(self_out, 0),
            halves(text_query[0], 1),
            own_out(text_out, 0),
            common(jnp.zeros((strip, 64), LOW)),
        )
    )
    piece_2 = spread(own_ff(0))
    piece_3 = spread(
        joined(
            own_text(1),
            own_out(self_out, 1),
            halves(text_query[1], 1),
            own_out(text_out, 1),
            own_in(1),
        )
    )
    piece_4 = spread(own_ff(1))

    w_in = [piece_0[:, :576], piece_3[:, 960:1536]]
    norm_rows = piece_0[:, 576:588].astype(FULL).T
    gains = [norm_rows[0:3], norm_rows[3:6]]
    shifts = [norm_rows[6:9], norm_rows[9:12]]
    w_text = [piece_1[:, :384], piece_3[:, :384]]
    memory_all = piece_1[:, 384:768]
    w_out = [piece_1[:, 768:960], piece_3[:, 384:576]]
    w_query = [piece_1[:, 960:1152], piece_3[:, 576:768]]
    w_tout = [piece_1[:, 1152:1344], piece_3[:, 768:960]]
    w_up = [piece_2[:, :ff], piece_4[:, :ff]]
    w_down = [piece_2[:, ff:], piece_4[:, ff:]]

    def own_rows(x):
        here = width_mixed(lax.dynamic_slice_in_dim(x, row * 16, 16, axis=1))
        keep = jnp.where(zh == 0, here[0], here[1])
        send = jnp.where(zh == 0, here[1], here[0])
        return jnp.concatenate([keep, swapped(send, "zh")], axis=0)

    token_rows = own_rows(tokens)
    grad_rows = own_rows(out_grad)

    at = jnp.arange(2048, dtype=jnp.int32)
    d_z, d_y, d_c = at // 1024, (at // 256) % 4, (at // 128) % 2
    d_x, d_s, inner = (at // 32) % 4, (at // 16) % 2, at % 16
    block = (zh ^ d_s) * 16 + (zl ^ d_z) * 8 + (xl ^ (d_x & 1)) * 4 + (y ^ d_y)
    key_at = block * 64 + ((xh ^ (d_x >> 1)) * 2 + (core ^ d_c)) * 16 + inner
    lengths = jnp.where(zh == 0, clip_lengths[0], clip_lengths[1])
    end_0 = lengths[0]
    end_1 = lengths[0] + lengths[1]
    key_clip = (key_at >= end_0).astype(jnp.int32) + (key_at >= end_1).astype(jnp.int32)
    frame_at, frame_clip = key_at[:256], key_clip[:256]
    allowed = (frame_clip[:, None] == key_clip[None, :]) & (key_at[None, :] <= frame_at[:, None])
    text_allowed = frame_clip[:, None] == (jnp.arange(192, dtype=jnp.int32) // 64)[None, :]

    token_all = rows_of_all(token_rows)
    unit_all, _ = unit(token_all.astype(FULL))
    residual = token_rows.astype(FULL)
    kept = []
    for l in range(2):
        n_0, r_0 = unit(residual)
        if l == 0:
            a = (unit_all * gains[0][0] + shifts[0][0]).astype(LOW)
        else:
            a = rows_of_all((n_0 * gains[l][0] + shifts[l][0]).astype(LOW))
        qkv = nn(a, w_in[l]).astype(LOW)
        q = qkv[:, :WIDE]
        kv = keys_of_all(qkv[:, WIDE:])
        k, v = kv[:, :WIDE], kv[:, WIDE:]
        o, lse = attend(q, k, v, allowed)
        x1 = residual + sum_to_rows(nt(o, w_out[l]))
        n_1, r_1 = unit(x1)
        c = rows_of_all((n_1 * gains[l][1] + shifts[l][1]).astype(LOW))
        cq = nn(c, w_query[l]).astype(LOW)
        mkv = tn(memory_all, w_text[l]).astype(LOW)
        mkv = jnp.where(zh == 0, mkv[:192], mkv[192:])
        mk, mv = mkv[:, :WIDE], mkv[:, WIDE:]
        co, clse = attend(cq, mk, mv, text_allowed)
        x2 = x1 + sum_to_rows(nt(co, w_tout[l]))
        n_2, r_2 = unit(x2)
        e = rows_of_all((n_2 * gains[l][2] + shifts[l][2]).astype(LOW))
        u = nn(e, w_up[l])
        hmid = gelu(u).astype(LOW)
        residual = x2 + sum_to_rows(nt(hmid, w_down[l]))
        kept.append((n_0, r_0, a, q, k, v, o, lse, n_1, r_1, c, cq, mk, mv, co, clse, n_2, r_2, e, u, hmid))

    def frames_back(rows):
        pair = rows.reshape(2, 16, width)
        other = swapped(pair[1], "zh")
        mbs = jnp.where(zh == 0, jnp.stack([pair[0], other]), jnp.stack([other, pair[0]]))
        mbs = width_restored(mbs)
        both = jnp.stack([mbs, swapped(mbs, "core")])
        both = jnp.where(core == 0, both, both[::-1])
        four = jnp.stack([both, swapped(both, "xh")])
        four = jnp.where(xh == 0, four, four[::-1])
        return jnp.moveaxis(four.reshape(4, 2, 16, width), 0, 1).reshape(2, 64, width)

    output = frames_back(residual.astype(LOW))

    grad = grad_rows.astype(FULL)
    norm_sums = [[None] * 3, [None] * 3]
    reduced = []
    memory_partial = jnp.zeros((width, 384), FULL)

    def norm_step(l, k, grad, upstream, n, r):
        norm_sums[l][k] = (jnp.sum(upstream * n, axis=0), jnp.sum(upstream, axis=0))
        return grad + unit_back(upstream, n, r, gains[l][k])

    def gathered_sum(parts):
        both = jnp.concatenate([p.astype(LOW) for p in parts], axis=1)
        return lax.psum_scatter(both, SPREAD, scatter_dimension=0, tiled=True)

    for l in (1, 0):
        n_0, r_0, a, q, k, v, o, lse, n_1, r_1, c, cq, mk, mv, co, clse, n_2, r_2, e, u, hmid = kept[l]
        dy = rows_of_all(grad.astype(LOW))
        g_down = tn(dy, hmid)
        du = (nn(dy, w_down[l]) * gelu_slope(u)).astype(LOW)
        g_up = tn(e, du)
        reduced.append(gathered_sum([g_up, g_down]))
        grad = norm_step(l, 2, grad, sum_to_rows(nt(du, w_up[l])), n_2, r_2)

        dy = rows_of_all(grad.astype(LOW))
        g_tout = tn(dy, co)
        dco = nn(dy, w_tout[l]).astype(LOW)
        dcq, dmk, dmv = attend_back(dco, cq, mk, mv, text_allowed, clse)
        dcq = dcq.astype(LOW)
        dmkv = jnp.concatenate([dmk, dmv], axis=1).astype(LOW)
        none = jnp.zeros_like(dmkv)
        dmkv = jnp.where(
            zh == 0, jnp.concatenate([dmkv, none]), jnp.concatenate([none, dmkv])
        )
        g_text = nn(memory_all, dmkv)
        memory_partial = memory_partial + nt(w_text[l], dmkv)
        g_query = tn(c, dcq)
        grad = norm_step(l, 1, grad, sum_to_rows(nt(dcq, w_query[l])), n_1, r_1)

        dy = rows_of_all(grad.astype(LOW))
        g_out = tn(dy, o)
        do = nn(dy, w_out[l]).astype(LOW)
        dq, dk, dv = attend_back(do, q, k, v, allowed, lse)
        if l == 0:
            reduced.append(
                gathered_sum([g_text, memory_partial, g_out, g_query, g_tout, jnp.zeros((width, 64), LOW)])
            )
        dkv = sum_to_keys(jnp.concatenate([dk, dv], axis=1))
        dqkv = jnp.concatenate([dq, dkv], axis=1).astype(LOW)
        g_in = tn(a, dqkv)
        da = nt(dqkv, w_in[l])
        if l == 1:
            reduced.append(gathered_sum([g_text, g_out, g_query, g_tout, g_in]))
            grad = norm_step(l, 0, grad, sum_to_rows(da), n_0, r_0)
        else:
            norm_sums[0][0] = (jnp.sum(da * unit_all, axis=0), jnp.sum(da, axis=0))
            sums = jnp.stack(
                [norm_sums[i][j][0] for i in range(2) for j in range(3)]
                + [norm_sums[i][j][1] for i in range(2) for j in range(3)]
            )
            sums = jnp.pad(sums.T, ((0, 0), (0, 52)))
            reduced.append(gathered_sum([g_in, sums]))
            grad = grad + unit_back(sum_to_rows(da), n_0, r_0, gains[0][0])
    input_grad = frames_back(grad.astype(LOW)).astype(FULL)

    ff_1, rest_1, ff_0, rest_0, in_0 = reduced

    def strips(block):
        pair = block.reshape(2, strip, -1)
        mine = jnp.where(xl == 0, pair[0], pair[1])
        theirs = swapped(jnp.where(xl == 0, pair[1], pair[0]), "xl")
        return (
            jnp.where(xl == 0, mine, theirs).astype(FULL),
            jnp.where(xl == 0, theirs, mine).astype(FULL),
        )

    def cut(pair, start, size):
        return [x[:, start : start + size] for x in pair]

    def wide(pair, start, size):
        return jnp.concatenate(cut(pair, start, size), axis=1)

    def tall(pair, start, size):
        return wide(pair, start, size).T

    def everywhere(x):
        x = x + swapped(x.astype(LOW), "core").astype(FULL)
        return x + swapped(x.astype(LOW), "xh").astype(FULL)

    ff_1, rest_1, ff_0, rest_0, in_0 = [strips(b) for b in (ff_1, rest_1, ff_0, rest_0, in_0)]
    self_in_grad = jnp.stack(
        [
            jnp.stack([wide(in_0, k * WIDE, WIDE) for k in range(3)]),
            jnp.stack([wide(rest_1, 960 + k * WIDE, WIDE) for k in range(3)]),
        ]
    )
    text_kv_grad = jnp.stack(
        [jnp.stack([wide(p, k * WIDE, WIDE) for k in range(2)]) for p in (rest_0, rest_1)]
    )
    self_out_grad = jnp.stack([tall(rest_0, 768, WIDE), tall(rest_1, 384, WIDE)])
    text_query_grad = jnp.stack([wide(rest_0, 960, WIDE), wide(rest_1, 576, WIDE)])
    text_out_grad = jnp.stack([tall(rest_0, 1152, WIDE), tall(rest_1, 768, WIDE)])
    mlp_up_grad = jnp.stack([wide(ff_0, 0, ff), wide(ff_1, 0, ff)])
    mlp_down_grad = jnp.stack([tall(ff_0, ff, ff), tall(ff_1, ff, ff)])
    memory_grad = everywhere(sum(cut(rest_0, 384, 384))).T.reshape(2, 192, strip)
    norm_grads = everywhere(sum(cut(in_0, 576, 64)))[:, :12].T
    gain_grad = norm_grads[:6].reshape(2, 3, strip)
    shift_grad = norm_grads[6:].reshape(2, 3, strip)
    return (
        output,
        input_grad,
        memory_grad,
        gain_grad,
        shift_grad[:, 0:2],
        shift_grad[:, 2],
        self_in_grad,
        self_out_grad,
        text_query_grad,
        text_kv_grad,
        text_out_grad,
        mlp_up_grad,
        mlp_down_grad,
    )


def solution(mesh):
    fine = Mesh(mesh.devices.reshape(FINE_SIZES), FINE)
    frames = P(None, COL, None)
    strips = P(None, None, COL)
    return jax.shard_map(
        local,
        mesh=fine,
        in_specs=(
            frames,
            strips,
            P(),
            frames,
            strips,
            strips,
            P(None, None, COL, ROW),
            P(None, ROW, COL),
            P(None, COL, ROW),
            P(None, None, COL, ROW),
            P(None, ROW, COL),
            P(None, COL, ROW),
            P(None, ROW, COL),
        ),
        out_specs=(
            frames,
            frames,
            strips,
            strips,
            strips,
            P(None, COL),
            P(None, None, COL, ROW),
            P(None, ROW, COL),
            P(None, COL, ROW),
            P(None, None, COL, ROW),
            P(None, ROW, COL),
            P(None, COL, ROW),
            P(None, ROW, COL),
        ),
        check_vma=False,
    )
```

```python
import math

import jax
import jax.numpy as jnp
from jax import lax
from jax.experimental import pallas as pl
from jax.experimental.pallas import tpu as pltpu
from jax.sharding import Mesh, PartitionSpec as P

HEAD = 64
HEADS_HERE = 3
WIDE = HEAD * HEADS_HERE
NEG_FILL = -1e30
NORM_EPS = 1e-05
SCALE = 1.0 / math.sqrt(HEAD)
LOW = jnp.bfloat16
FULL = jnp.float32

FINE = ("xh", "core", "zh", "zl", "xl", "y")
FINE_SIZES = (2, 2, 2, 2, 2, 4)
ROW = ("xh", "core")
COL = ("zh", "zl", "xl", "y")
CHIPS = ("xh", "xl")
SPREAD = ("y", "zh", "zl")
DEEP = ("zh", "zl")
KEYED = ("zl", "y")
SWAP = ((0, 1), (1, 0))


def flipped(size, mask):
    return [(i, i ^ mask) for i in range(size)]


def swapped(x, axis):
    return lax.ppermute(x, axis, SWAP)


def rows_of_all(rows):
    chips = [rows] + [lax.ppermute(rows, CHIPS, flipped(4, d)) for d in (1, 2, 3)]
    half = jnp.concatenate(chips, axis=0)
    return jnp.concatenate([half, swapped(half, "core")], axis=0)


def sum_to_rows(partial):
    count = partial.shape[0] // 8
    blocks = partial.reshape(2, 4, count, partial.shape[1])
    both = blocks[0].astype(FULL) + swapped(blocks[1].astype(LOW), "core").astype(FULL)
    low = both.astype(LOW)
    total = both[0]
    for d in (1, 2, 3):
        total = total + lax.ppermute(low[d], CHIPS, flipped(4, d)).astype(FULL)
    return total


def keys_of_all(block):
    parts = [block]
    for d in range(1, 8):
        parts.append(lax.ppermute(block, KEYED, flipped(8, d)))
    return jnp.concatenate(parts, axis=0)


def sum_to_keys(partial):
    blocks = partial.reshape(8, -1, partial.shape[1])
    low = blocks.astype(LOW)
    total = blocks[0].astype(FULL)
    for d in range(1, 8):
        total = total + lax.ppermute(low[d], KEYED, flipped(8, d)).astype(FULL)
    return total


def sum_to_strips(partial):
    y = lax.axis_index("y")
    z = lax.axis_index("zh") * 2 + lax.axis_index("zl")

    def level(values, axis, here, order):
        low = values.astype(LOW)
        count = values.shape[0] // 4

        def block(x, d):
            return lax.dynamic_slice_in_dim(x, (here ^ d) * count, count, axis=0)

        total = block(values, 0).astype(FULL)
        for d in order:
            total = total + lax.ppermute(block(low, d), axis, flipped(4, d)).astype(FULL)
        return total

    return level(level(partial, "y", y, (1, 3, 2)), DEEP, z, (1, 3, 2)).astype(LOW)


def tied(*arrays):
    return lax.optimization_barrier(arrays)


def mm(a, b, dims):
    return lax.dot_general(a, b, (dims, ((), ())), preferred_element_type=FULL)


def nn(a, b):
    return mm(a, b, ((1,), (0,)))


def nt(a, b):
    return mm(a, b, ((1,), (1,)))


def tn(a, b):
    return mm(a, b, ((0,), (0,)))


def unit(values):
    centre = jnp.mean(values, axis=-1, keepdims=True)
    centred = values - centre
    inverse = lax.rsqrt(jnp.mean(centred * centred, axis=-1, keepdims=True) + NORM_EPS)
    return centred * inverse, inverse


def unit_back(upstream, unit_rows, inverse, gain_row):
    scaled = upstream * gain_row
    inner = (
        scaled
        - jnp.mean(scaled, axis=-1, keepdims=True)
        - unit_rows * jnp.mean(scaled * unit_rows, axis=-1, keepdims=True)
    )
    return inner * inverse


def whole(x):
    return pl.BlockSpec(x.shape, lambda i: (0,) * x.ndim)


def window(columns, index, rows=None):
    return lambda x: pl.BlockSpec((x.shape[0], columns), lambda i: (0, index))


def kernel_call(body, args, outs, steps=1, specs=None, out_specs=None):
    shapes = [jax.ShapeDtypeStruct(shape, kind) for shape, kind in outs]
    placed = [(spec or whole)(x) for x, spec in zip(args, specs or [None] * len(args))]
    return pl.pallas_call(
        body,
        grid=(steps,),
        in_specs=placed,
        out_specs=out_specs or [whole(x) for x in shapes],
        out_shape=shapes,
        compiler_params=pltpu.CompilerParams(vmem_limit_bytes=48 * 2**20),
    )(*args)


def head(x, h, start=0):
    return x[:, start + h * HEAD : start + (h + 1) * HEAD]


def attend_into(q, kv, bias, o_ref, lse_ref):
    rows = []
    for h in range(HEADS_HERE):
        s = nt(head(kv, h), head(q, h)) * SCALE + bias
        top = jnp.max(s, axis=0, keepdims=True)
        lse = top + jnp.log(jnp.sum(jnp.exp(s - top), axis=0, keepdims=True))
        p = jnp.exp(s - lse).astype(LOW)
        lse_ref[h : h + 1, :] = lse
        rows.append(tn(head(kv, h, WIDE), p))
    lse_ref[HEADS_HERE:, :] = jnp.zeros((8 - HEADS_HERE, lse_ref.shape[1]), FULL)
    o = jnp.concatenate(rows, axis=0).T.astype(LOW)
    o_ref[...] = o
    return o


def attend_back(do, q, kv, bias, lse_ref):
    dqs, dks, dvs = [], [], []
    for h in range(HEADS_HERE):
        k, v, q_h, do_h = head(kv, h), head(kv, h, WIDE), head(q, h), head(do, h)
        p = jnp.exp(nt(k, q_h) * SCALE + bias - lse_ref[h : h + 1, :])
        dp = nt(v, do_h)
        inner = jnp.sum(p * dp, axis=0, keepdims=True)
        ds = (p * (dp - inner)).astype(LOW)
        dqs.append(tn(k, ds) * SCALE)
        dks.append(nn(ds, q_h) * SCALE)
        dvs.append(nn(p.astype(LOW), do_h))
    dq = jnp.concatenate(dqs, axis=0).T
    return dq, jnp.concatenate(dks + dvs, axis=1)


def self_forward(q_ref, kv_ref, bias_ref, w_ref, o_ref, lse_ref, out_ref):
    q = q_ref[...][:, :WIDE]
    o = attend_into(q, kv_ref[...], bias_ref[...], o_ref, lse_ref)
    out_ref[...] = nt(o, w_ref[...][:, :WIDE]).astype(LOW)


def cross_forward(c_ref, kv_ref, bias_ref, wq_ref, wo_ref, q_ref, o_ref, lse_ref, out_ref):
    q = nn(c_ref[...], wq_ref[...][:, WIDE : 2 * WIDE]).astype(LOW)
    q_ref[...] = q
    o = attend_into(q, kv_ref[...], bias_ref[...], o_ref, lse_ref)
    out_ref[...] = nt(o, wo_ref[...][:, :WIDE]).astype(LOW)


def self_backward(dy_ref, q_ref, kv_ref, bias_ref, lse_ref, w_ref, dq_ref, dkv_ref):
    do = nn(dy_ref[...], w_ref[...][:, :WIDE]).astype(LOW)
    dq, dkv = attend_back(do, q_ref[...][:, :WIDE], kv_ref[...], bias_ref[...], lse_ref)
    dq_ref[...] = dq.astype(LOW)
    dkv_ref[...] = dkv.astype(LOW)


def cross_backward(
    dy_ref, q_ref, kv_ref, bias_ref, lse_ref, wq_ref, wo_ref, dq_ref, dkv_ref, out_ref
):
    do = nn(dy_ref[...], wo_ref[...][:, :WIDE]).astype(LOW)
    dq, dkv = attend_back(do, q_ref[...], kv_ref[...], bias_ref[...], lse_ref)
    dq = dq.astype(LOW)
    dq_ref[...] = dq
    dkv_ref[...] = dkv.astype(LOW)
    out_ref[...] = nt(dq, wq_ref[...][:, WIDE : 2 * WIDE]).astype(LOW)


def ff_forward(e_ref, up_ref, down_ref, u_ref, hmid_ref, out_ref):
    u = nn(e_ref[...], up_ref[...])
    hmid = gelu(u).astype(LOW)
    u_ref[...] = u
    hmid_ref[...] = hmid
    out_ref[...] = nt(hmid, down_ref[...]).astype(LOW)


def ff_backward(dy_ref, u_ref, up_ref, down_ref, du_ref, out_ref):
    du = (nn(dy_ref[...], down_ref[...]) * gelu_slope(u_ref[...])).astype(LOW)
    du_ref[...] = du
    out_ref[...] = nt(du, up_ref[...]).astype(LOW)


def weight_sums(groups, width):
    steps, args, specs, plan, columns = 4, [], [], [], 0
    rows = width // steps

    def put(x, spec):
        args.append(x)
        specs.append(spec)
        return len(args) - 1

    for group in groups:
        terms = []
        size = 0
        for kind, a, b in group:
            if kind == "tn":
                at = put(a, lambda x: pl.BlockSpec((x.shape[0], rows), lambda i: (0, i)))
                size += b.shape[1]
            else:
                cut, index = a[1]
                at = put(a[0], lambda x, c=cut, k=index: pl.BlockSpec((rows, c), lambda i: (i, k)))
                size = b.shape[0] if kind == "nt" else b.shape[1]
            terms.append((kind, at, put(b, None)))
        plan.append((columns, size, terms))
        columns += size

    def body(*refs):
        out_ref = refs[-1]
        for start, size, terms in plan:
            if terms[0][0] == "tn":
                parts = [tn(refs[a][...], refs[b][...]) for _, a, b in terms]
                value = parts[0] if len(parts) == 1 else jnp.concatenate(parts, axis=1)
            else:
                product = nt if terms[0][0] == "nt" else nn
                value = sum(product(refs[a][...], refs[b][...]) for _, a, b in terms)
            out_ref[:, start : start + size] = value.astype(LOW)

    return kernel_call(
        body,
        args,
        [((width, columns), LOW)],
        steps,
        specs,
        [pl.BlockSpec((rows, columns), lambda i: (i, 0))],
    )[0]


def laid_out(parts, here, strip, ff):
    early, first, last = parts
    args = [here.reshape(1), *early, *first, *last]

    def body(*refs):
        lower = refs[0][0] == 0
        kept = []
        for mine, theirs in ((1, 2), (3, 4), (5, 6)):
            a, b = refs[mine][...].astype(FULL), refs[theirs][...].astype(FULL)
            kept.append((jnp.where(lower, a, b), jnp.where(lower, b, a)))
        early, first, last = kept
        g_in, g_out, g_query, g_text, g_tout, g_up, g_down = refs[7:]

        def wide(pair, start, size):
            return jnp.concatenate([x[:, start : start + size] for x in pair], axis=1)

        for k in range(3):
            g_in[0, k] = wide(last, k * WIDE, WIDE)
            g_in[1, k] = wide(first, 2688 + k * WIDE, WIDE)
        g_out[0] = wide(last, 576, WIDE)
        g_out[1] = wide(first, 3264, WIDE)
        for l, pair in enumerate((first, early)):
            g_up[l] = wide(pair, 0, ff)
            g_down[l] = wide(pair, ff, ff)
            for k in range(2):
                g_text[l, k] = wide(pair, 1536 + k * WIDE, WIDE)
            g_query[l] = wide(pair, 1920, WIDE)
            g_tout[l] = wide(pair, 2112, WIDE)

    outs = [
        ((2, 3, strip, 2 * WIDE), FULL),
        ((2, strip, 2 * WIDE), FULL),
        ((2, strip, 2 * WIDE), FULL),
        ((2, 2, strip, 2 * WIDE), FULL),
        ((2, strip, 2 * WIDE), FULL),
        ((2, strip, 2 * ff), FULL),
        ((2, strip, 2 * ff), FULL),
    ]
    specs = [lambda x: pl.BlockSpec(memory_space=pltpu.SMEM)] + [None] * 6
    return kernel_call(body, args, outs, 1, specs)


def gelu(z):
    return 0.5 * z * (1.0 + lax.erf(z * math.sqrt(0.5)))


def gelu_slope(z):
    half = 0.5 * (1.0 + lax.erf(z * math.sqrt(0.5)))
    return half + z * jnp.exp(-0.5 * z * z) * (1.0 / math.sqrt(2.0 * math.pi))


def width_mixed(x):
    lead = x.shape[:-1]
    parts = x.reshape(*lead, 8, 4, -1)
    return jnp.swapaxes(parts, -2, -3).reshape(*lead, -1)


def width_restored(x):
    lead = x.shape[:-1]
    parts = x.reshape(*lead, 4, 8, -1)
    return jnp.swapaxes(parts, -2, -3).reshape(*lead, -1)


def local(
    tokens,
    memory,
    clip_lengths,
    out_grad,
    norm_gain,
    norm_bias,
    self_in,
    self_out,
    text_query,
    text_kv,
    text_out,
    mlp_up,
    mlp_down,
):
    xh, core, zh = lax.axis_index("xh"), lax.axis_index("core"), lax.axis_index("zh")
    zl, xl, y = lax.axis_index("zl"), lax.axis_index("xl"), lax.axis_index("y")
    row = xh * 2 + core
    width = tokens.shape[2]
    strip = memory.shape[2]
    ff = mlp_up.shape[2] // 2

    def halves(x, axis):
        size = x.shape[axis] // 2
        a = lax.slice_in_dim(x, 0, size, axis=axis)
        b = lax.slice_in_dim(x, size, 2 * size, axis=axis)
        return a, b

    def joined(*pairs):
        return tuple(jnp.concatenate(side, axis=1) for side in zip(*pairs))

    def common(x):
        return x, x

    def strips_of_pair(pair):
        first, second = pair
        mine = jnp.where(xl == 0, first, second)
        theirs = swapped(jnp.where(xl == 0, second, first), "xl")
        return jnp.where(
            xl == 0, jnp.concatenate([mine, theirs]), jnp.concatenate([theirs, mine])
        )

    def spread(pair):
        return lax.all_gather(strips_of_pair(pair), SPREAD, axis=0, tiled=True)

    def spread_now(own):
        sent = jnp.broadcast_to(own[None], (16, *own.shape))
        return lax.all_to_all(sent, SPREAD, 0, 0, tiled=True).reshape(-1, own.shape[1])

    norms = jnp.concatenate([norm_gain.reshape(6, strip), norm_bias.reshape(6, strip)])
    norms = jnp.pad(norms.T, ((0, 0), (0, 52)))
    memory_t = memory.reshape(-1, strip).T

    def own_in(l):
        return joined(*[halves(self_in[l, k], 1) for k in range(3)])

    def own_out(w, l):
        return halves(w[l].T, 1)

    def own_text(l):
        return joined(*[halves(text_kv[l, k], 1) for k in range(2)])

    def own_ff(l):
        return joined(halves(mlp_up[l], 1), own_out(mlp_down, l))

    own_0 = strips_of_pair(joined(own_in(0), common(norms)))
    own_0, self_out, text_query, text_kv, text_out, memory_t = tied(
        own_0, self_out, text_query, text_kv, text_out, memory_t
    )
    piece_0 = spread_now(own_0)
    piece_1 = spread(
        joined(
            own_text(0),
            common(memory_t),
            own_out(self_out, 0),
            halves(text_query[0], 1),
            own_out(text_out, 0),
            common(jnp.zeros((strip, 192), LOW)),
        )
    )
    piece_2 = spread(
        joined(
            own_ff(0),
            own_text(1),
            own_out(self_out, 1),
            halves(text_query[1], 1),
            own_out(text_out, 1),
            own_in(1),
        )
    )
    piece_3 = spread(own_ff(1))

    w_in = [piece_0[:, :576], piece_2[:, 2496:3072]]
    norm_rows = piece_0[:, 576:588].astype(FULL).T
    gains = [norm_rows[0:3], norm_rows[3:6]]
    shifts = [norm_rows[6:9], norm_rows[9:12]]
    attn = [piece_1, piece_2]
    feed = [piece_2, piece_3]
    w_text = [piece_1[:, :384], piece_2[:, 1536:1920]]
    memory_all = piece_1[:, 384:768]
    up_window, down_window = window(ff, 0), window(ff, 1)
    mixed_window = [window(384, 2), window(384, 5)]
    tout_window = [window(384, 3), window(768, 3)]

    def own_rows(x):
        here = width_mixed(lax.dynamic_slice_in_dim(x, row * 16, 16, axis=1))
        keep = jnp.where(zh == 0, here[0], here[1])
        send = jnp.where(zh == 0, here[1], here[0])
        return jnp.concatenate([keep, swapped(send, "zh")], axis=0)

    token_rows = own_rows(tokens)
    grad_rows = own_rows(out_grad)

    at = jnp.arange(2048, dtype=jnp.int32)
    d_z, d_y, d_c = at // 1024, (at // 256) % 4, (at // 128) % 2
    d_x, d_s, inner = (at // 32) % 4, (at // 16) % 2, at % 16
    block = (zh ^ d_s) * 16 + (zl ^ d_z) * 8 + (xl ^ (d_x & 1)) * 4 + (y ^ d_y)
    key_at = block * 64 + ((xh ^ (d_x >> 1)) * 2 + (core ^ d_c)) * 16 + inner
    lengths = jnp.where(zh == 0, clip_lengths[0], clip_lengths[1])
    end_0 = lengths[0]
    end_1 = lengths[0] + lengths[1]
    key_clip = (key_at >= end_0).astype(jnp.int32) + (key_at >= end_1).astype(jnp.int32)
    frame_at, frame_clip = key_at[:256], key_clip[:256]
    allowed = (frame_clip[None, :] == key_clip[:, None]) & (key_at[:, None] <= frame_at[None, :])
    bias = jnp.where(allowed, 0.0, NEG_FILL).astype(FULL)
    text_clip = jnp.arange(192, dtype=jnp.int32) // 64
    text_bias = jnp.where(frame_clip[None, :] == text_clip[:, None], 0.0, NEG_FILL).astype(FULL)
    frames = bias.shape[1]
    low_frames = ((frames, WIDE), LOW)
    lse_rows = ((8, frames), FULL)
    partial_rows = ((frames, width), LOW)

    token_all = rows_of_all(token_rows)
    unit_all, _ = unit(token_all.astype(FULL))
    residual = token_rows.astype(FULL)
    kept = []
    for l in range(2):
        n_0, r_0 = unit(residual)
        if l == 0:
            a = (unit_all * gains[0][0] + shifts[0][0]).astype(LOW)
        else:
            a = rows_of_all((n_0 * gains[l][0] + shifts[l][0]).astype(LOW))
        qkv = nn(a, w_in[l]).astype(LOW)
        kv = keys_of_all(qkv[:, WIDE:])
        o, lse, part = kernel_call(
            self_forward,
            [qkv, kv, bias, attn[l]],
            [low_frames, lse_rows, partial_rows],
            specs=[None, None, None, mixed_window[l]],
        )
        x1 = residual + sum_to_rows(part)
        n_1, r_1 = unit(x1)
        c = rows_of_all((n_1 * gains[l][1] + shifts[l][1]).astype(LOW))
        mkv = tn(memory_all, w_text[l]).astype(LOW)
        mkv = jnp.where(zh == 0, mkv[:192], mkv[192:])
        cq, co, clse, part = kernel_call(
            cross_forward,
            [c, mkv, text_bias, attn[l], attn[l]],
            [low_frames, low_frames, lse_rows, partial_rows],
            specs=[None, None, None, mixed_window[l], tout_window[l]],
        )
        x2 = x1 + sum_to_rows(part)
        n_2, r_2 = unit(x2)
        e = rows_of_all((n_2 * gains[l][2] + shifts[l][2]).astype(LOW))
        u, hmid, part = kernel_call(
            ff_forward,
            [e, feed[l], feed[l]],
            [((frames, ff), FULL), ((frames, ff), LOW), partial_rows],
            specs=[None, up_window, down_window],
        )
        residual = x2 + sum_to_rows(part)
        kept.append((n_0, r_0, a, qkv, kv, o, lse, n_1, r_1, c, cq, mkv, co, clse, n_2, r_2, e, u, hmid))

    def frames_back(rows):
        pair = rows.reshape(2, 16, width)
        other = swapped(pair[1], "zh")
        mbs = jnp.where(zh == 0, jnp.stack([pair[0], other]), jnp.stack([other, pair[0]]))
        mbs = width_restored(mbs)
        both = jnp.stack([mbs, swapped(mbs, "core")])
        both = jnp.where(core == 0, both, both[::-1])
        four = jnp.stack([both, swapped(both, "xh")])
        four = jnp.where(xh == 0, four, four[::-1])
        return jnp.moveaxis(four.reshape(4, 2, 16, width), 0, 1).reshape(2, 64, width)

    output = frames_back(residual.astype(LOW))

    grad = grad_rows.astype(FULL)
    norm_sums = [[None] * 3, [None] * 3]
    memory_partial = jnp.zeros((width, 384), FULL)

    def norm_step(l, k, grad, upstream, n, r):
        norm_sums[l][k] = (jnp.sum(upstream * n, axis=0), jnp.sum(upstream, axis=0))
        return grad + unit_back(upstream, n, r, gains[l][k])

    def summed(both):
        return lax.psum_scatter(both, SPREAD, scatter_dimension=0, tiled=True)

    memory_terms = []
    for l in (1, 0):
        n_0, r_0, a, qkv, kv, o, lse, n_1, r_1, c, cq, mkv, co, clse, n_2, r_2, e, u, hmid = kept[l]
        dy = rows_of_all(grad.astype(LOW))
        du, part = kernel_call(
            ff_backward,
            [dy, u, feed[l], feed[l]],
            [((frames, ff), LOW), partial_rows],
            specs=[None, None, up_window, down_window],
        )
        de = sum_to_rows(part)
        groups = [[("tn", e, du)], [("tn", dy, hmid)]]
        grad = norm_step(l, 2, grad, de, n_2, r_2)

        dy = rows_of_all(grad.astype(LOW))
        dcq, dmkv, part = kernel_call(
            cross_backward,
            [dy, cq, mkv, text_bias, clse, attn[l], attn[l]],
            [low_frames, ((192, 2 * WIDE), LOW), partial_rows],
            specs=[None] * 5 + [mixed_window[l], tout_window[l]],
        )
        dc = sum_to_rows(part)
        none = jnp.zeros_like(dmkv)
        dmkv = jnp.where(
            zh == 0, jnp.concatenate([dmkv, none]), jnp.concatenate([none, dmkv])
        )
        memory_terms.append(("nt", (attn[l], (384, 4 * l)), dmkv))
        groups += [[("nn", (piece_1, (384, 1)), dmkv)], [("tn", c, dcq), ("tn", dy, co)]]
        if l == 0:
            groups += [memory_terms] + late
        first = weight_sums(groups, width)
        dc, first = tied(dc, first)
        first = summed(first)
        if l == 0:
            dc, early = tied(dc, early)
        grad = norm_step(l, 1, grad, dc, n_1, r_1)

        dy = rows_of_all(grad.astype(LOW))
        dq, dkv = kernel_call(
            self_backward,
            [dy, qkv, kv, bias, lse, attn[l]],
            [low_frames, ((kv.shape[0], 2 * WIDE), LOW)],
            specs=[None] * 5 + [mixed_window[l]],
        )
        dkv = sum_to_keys(dkv)
        dqkv = jnp.concatenate([dq, dkv.astype(LOW)], axis=1)
        da = nt(dqkv, w_in[l])
        late = [[("tn", a, dqkv), ("tn", dy, o)]]
        if l == 1:
            grad = norm_step(l, 0, grad, sum_to_rows(da), n_0, r_0)
            early = first
        else:
            norm_sums[0][0] = (jnp.sum(da * unit_all, axis=0), jnp.sum(da, axis=0))
            last = sum_to_strips(weight_sums(late, width))
            sums = jnp.stack(
                [norm_sums[i][j][0] for i in range(2) for j in range(3)]
                + [norm_sums[i][j][1] for i in range(2) for j in range(3)]
            )
            sums = jnp.pad(sums, ((0, 4), (0, 0)))
            extra = jnp.broadcast_to(sums[None], (8, *sums.shape))
            da = jnp.concatenate([da.reshape(8, -1, width), extra], axis=1)
            da = sum_to_rows(da.reshape(-1, width))
            norm_total = da[-16:].astype(LOW).reshape(16, 16, -1)
            norm_total = lax.all_to_all(jnp.swapaxes(norm_total, 0, 1), SPREAD, 0, 0, tiled=True)
            norm_total = jnp.sum(norm_total.astype(FULL), axis=0)
            grad = grad + unit_back(da[:-16], n_0, r_0, gains[0][0])
    input_grad = frames_back(grad.astype(LOW)).astype(FULL)

    def strips(block):
        mine = lax.dynamic_slice_in_dim(block, xl * strip, strip, axis=0)
        theirs = lax.dynamic_slice_in_dim(block, (1 - xl) * strip, strip, axis=0)
        return mine, swapped(theirs, "xl")

    def both(pair, start, size):
        return sum(x[:, start : start + size].astype(FULL) for x in pair)

    def everywhere(x):
        x = x + swapped(x.astype(LOW), "core").astype(FULL)
        return x + swapped(x.astype(LOW), "xh").astype(FULL)

    early, first, last = [strips(b) for b in (early, first, last)]
    laid = laid_out((early, first, last), xl, strip, ff)
    self_in_grad, self_out_grad, text_query_grad, text_kv_grad = laid[:4]
    text_out_grad, mlp_up_grad, mlp_down_grad = laid[4:]
    self_out_grad, text_out_grad, mlp_down_grad = [
        jnp.swapaxes(x, 1, 2) for x in (self_out_grad, text_out_grad, mlp_down_grad)
    ]
    memory_grad = everywhere(both(first, 2304, 384)).reshape(strip, 2, 192)
    memory_grad = jnp.transpose(memory_grad, (1, 2, 0))
    norm_grads = lax.dynamic_slice_in_dim(norm_total, xl * strip, strip, axis=1)
    gain_grad = norm_grads[:6].reshape(2, 3, strip)
    shift_grad = norm_grads[6:12].reshape(2, 3, strip)
    return (
        output,
        input_grad,
        memory_grad,
        gain_grad,
        shift_grad[:, 0:2],
        shift_grad[:, 2],
        self_in_grad,
        self_out_grad,
        text_query_grad,
        text_kv_grad,
        text_out_grad,
        mlp_up_grad,
        mlp_down_grad,
    )


def solution(mesh):
    fine = Mesh(mesh.devices.reshape(FINE_SIZES), FINE)
    frames = P(None, COL, None)
    strips = P(None, None, COL)
    return jax.shard_map(
        local,
        mesh=fine,
        in_specs=(
            frames,
            strips,
            P(),
            frames,
            strips,
            strips,
            P(None, None, COL, ROW),
            P(None, ROW, COL),
            P(None, COL, ROW),
            P(None, None, COL, ROW),
            P(None, ROW, COL),
            P(None, COL, ROW),
            P(None, ROW, COL),
        ),
        out_specs=(
            frames,
            frames,
            strips,
            strips,
            strips,
            P(None, COL),
            P(None, None, COL, ROW),
            P(None, ROW, COL),
            P(None, COL, ROW),
            P(None, None, COL, ROW),
            P(None, ROW, COL),
            P(None, COL, ROW),
            P(None, ROW, COL),
        ),
        check_vma=False,
    )
```

```python
import math

import jax
import jax.numpy as jnp
from jax import lax
from jax.experimental import pallas as pl
from jax.experimental.pallas import tpu as pltpu
from jax.sharding import Mesh, PartitionSpec as P

HEAD = 64
HEADS_HERE = 3
WIDE = HEAD * HEADS_HERE
NEG_FILL = -1e30
NORM_EPS = 1e-05
SCALE = 1.0 / math.sqrt(HEAD)
LOW = jnp.bfloat16
FULL = jnp.float32

FINE = ("xh", "core", "zh", "zl", "xl", "y")
FINE_SIZES = (2, 2, 2, 2, 2, 4)
ROW = ("xh", "core")
COL = ("zh", "zl", "xl", "y")
CHIPS = ("xh", "xl")
SPREAD = ("y", "zh", "zl")
DEEP = ("zh", "zl")
KEYED = ("zl", "y")
SWAP = ((0, 1), (1, 0))


def flipped(size, mask):
    return [(i, i ^ mask) for i in range(size)]


def swapped(x, axis):
    return lax.ppermute(x, axis, SWAP)


def rows_of_all(rows):
    chips = [rows] + [lax.ppermute(rows, CHIPS, flipped(4, d)) for d in (1, 2, 3)]
    half = jnp.concatenate(chips, axis=0)
    return [half, swapped(half, "core")]


def sum_to_rows(partial):
    count = partial.shape[0] // 8
    blocks = partial.reshape(2, 4, count, partial.shape[1])
    both = blocks[0].astype(FULL) + swapped(blocks[1].astype(LOW), "core").astype(FULL)
    low = both.astype(LOW)
    total = both[0]
    for d in (1, 2, 3):
        total = total + lax.ppermute(low[d], CHIPS, flipped(4, d)).astype(FULL)
    return total


def keys_pair(block):
    return jnp.concatenate([block, swapped(block, "zl")], axis=0)


def keys_of_all(pair):
    return [pair] + [lax.ppermute(pair, "y", flipped(4, d)) for d in (1, 2, 3)]


def keyed_mask(d):
    return (d & 1) * 4 + d // 2


def keyed_of_all(block):
    return [block] + [
        lax.ppermute(block, KEYED, flipped(8, keyed_mask(d))) for d in range(1, 8)
    ]


def strips_of_all(own):
    y = lax.axis_index("y")
    z = lax.axis_index("zh") * 2 + lax.axis_index("zl")
    places = {"y": (0, y), DEEP: (1, z)}
    rows = own.shape[0] // 2

    def level(x, axis):
        at, here = places[axis]
        shape = list(x.shape)
        shape[at] = 4
        out = jnp.zeros(shape, x.dtype)
        out = lax.dynamic_update_slice_in_dim(out, x, here, axis=at)
        for d in (1, 3, 2):
            part = lax.ppermute(x, axis, flipped(4, d))
            out = lax.dynamic_update_slice_in_dim(out, part, here ^ d, axis=at)
        return out

    halves = own.reshape(1, 1, 2, rows, -1)
    first = level(level(halves[:, :, 0], DEEP), "y")
    second = level(level(halves[:, :, 1], "y"), DEEP)
    return jnp.stack([first, second], axis=2).reshape(32 * rows, -1)


def strip_blocks(partial):
    return partial.reshape(4, 4, partial.shape[0] // 16, -1)


def sum_along(values, axis):
    if axis == "y":
        at, here = 0, lax.axis_index("y")
    else:
        at, here = 1, lax.axis_index("zh") * 2 + lax.axis_index("zl")
    low = values.astype(LOW)

    def block(x, d):
        return lax.dynamic_slice_in_dim(x, here ^ d, 1, axis=at)

    total = block(values, 0).astype(FULL)
    for d in (1, 3, 2):
        total = total + lax.ppermute(block(low, d), axis, flipped(4, d)).astype(FULL)
    return total


def strip_of(total):
    return total.reshape(-1, total.shape[-1]).astype(LOW)


def tied(*arrays):
    return lax.optimization_barrier(arrays)


def mm(a, b, dims):
    return lax.dot_general(a, b, (dims, ((), ())), preferred_element_type=FULL)


def nn(a, b):
    return mm(a, b, ((1,), (0,)))


def nt(a, b):
    return mm(a, b, ((1,), (1,)))


def tn(a, b):
    return mm(a, b, ((0,), (0,)))


def unit(values):
    centre = jnp.mean(values, axis=-1, keepdims=True)
    centred = values - centre
    inverse = lax.rsqrt(jnp.mean(centred * centred, axis=-1, keepdims=True) + NORM_EPS)
    return centred * inverse, inverse


def unit_back(upstream, unit_rows, inverse, gain_row):
    scaled = upstream * gain_row
    inner = (
        scaled
        - jnp.mean(scaled, axis=-1, keepdims=True)
        - unit_rows * jnp.mean(scaled * unit_rows, axis=-1, keepdims=True)
    )
    return inner * inverse


def whole(x):
    return pl.BlockSpec(x.shape, lambda i: (0,) * x.ndim)


def window(columns, index, rows=None):
    return lambda x: pl.BlockSpec((x.shape[0], columns), lambda i: (0, index))


def kernel_call(body, args, outs, steps=1, specs=None, out_specs=None, room=16):
    shapes = [jax.ShapeDtypeStruct(shape, kind) for shape, kind in outs]
    placed = [(spec or whole)(x) for x, spec in zip(args, specs or [None] * len(args))]
    return pl.pallas_call(
        body,
        grid=(steps,),
        in_specs=placed,
        out_specs=out_specs or [whole(x) for x in shapes],
        out_shape=shapes,
        compiler_params=pltpu.CompilerParams(vmem_limit_bytes=room * 2**20),
    )(*args)


def stacked(refs):
    return jnp.concatenate([ref[...] for ref in refs], axis=0)


def head(x, h, start=0):
    return x[:, start + h * HEAD : start + (h + 1) * HEAD]


def attend_into(q, kv, bias, o_ref, lse_ref):
    rows = []
    for h in range(HEADS_HERE):
        s = nt(head(kv, h), head(q, h)) * SCALE + bias
        top = jnp.max(s, axis=0, keepdims=True)
        lse = top + jnp.log(jnp.sum(jnp.exp(s - top), axis=0, keepdims=True))
        p = jnp.exp(s - lse).astype(LOW)
        lse_ref[h : h + 1, :] = lse
        rows.append(tn(head(kv, h, WIDE), p))
    lse_ref[HEADS_HERE:, :] = jnp.zeros((8 - HEADS_HERE, lse_ref.shape[1]), FULL)
    o = jnp.concatenate(rows, axis=0).T.astype(LOW)
    o_ref[...] = o
    return o


def packed(values, stats):
    columns = stats.T
    high = columns.astype(LOW)
    rest = columns - high.astype(FULL)
    middle = rest.astype(LOW)
    low = (rest - middle.astype(FULL)).astype(LOW)
    spare = jnp.zeros((values.shape[0], 256 - values.shape[1] - 3 * 8), LOW)
    return jnp.concatenate([values, high, middle, low, spare], axis=1)


def stats_of(pack):
    turned = pack[:, 128:256].astype(FULL).T
    return turned[64:72] + turned[72:80] + turned[80:88]


def attend_back(do, q, kv, bias, lse_ref):
    dqs, dks, dvs = [], [], []
    for h in range(HEADS_HERE):
        k, v, q_h, do_h = head(kv, h), head(kv, h, WIDE), head(q, h), head(do, h)
        p = jnp.exp(nt(k, q_h) * SCALE + bias - lse_ref[h : h + 1, :])
        dp = nt(v, do_h)
        inner = jnp.sum(p * dp, axis=0, keepdims=True)
        ds = (p * (dp - inner)).astype(LOW)
        dqs.append(tn(k, ds) * SCALE)
        dks.append(nn(ds, q_h) * SCALE)
        dvs.append(nn(p.astype(LOW), do_h))
    dq = jnp.concatenate(dqs, axis=0).T
    return dq, jnp.concatenate(dks + dvs, axis=1)


def project(a0_ref, a1_ref, w_ref, out_ref):
    out_ref[...] = nn(stacked((a0_ref, a1_ref)), w_ref[...][:, WIDE:]).astype(LOW)


def self_forward(q_ref, kv0, kv1, kv2, kv3, bias_ref, w_ref, o_ref, lse_ref, pack_ref, out_ref):
    q = q_ref[...][:, :WIDE]
    o = attend_into(q, stacked((kv0, kv1, kv2, kv3)), bias_ref[...], o_ref, lse_ref)
    pack_ref[...] = packed(q, lse_ref[...])
    out_ref[...] = nt(o, w_ref[...][:, :WIDE]).astype(LOW)


def cross_forward(c0_ref, c1_ref, kv_ref, bias_ref, w_ref, q_ref, o_ref, lse_ref, out_ref):
    q = nn(stacked((c0_ref, c1_ref)), w_ref[...][:, :WIDE]).astype(LOW)
    q_ref[...] = q
    o = attend_into(q, kv_ref[...], bias_ref[...], o_ref, lse_ref)
    out_ref[...] = nt(o, w_ref[...][:, WIDE:]).astype(LOW)


def self_upstream(dy0_ref, dy1_ref, o_ref, w_ref, pack_ref, delta_ref):
    do = nn(stacked((dy0_ref, dy1_ref)), w_ref[...][:, :WIDE]).astype(LOW)
    product = (do.astype(FULL) * o_ref[...].astype(FULL)).T
    sums = [
        jnp.sum(product[h * HEAD : (h + 1) * HEAD], axis=0, keepdims=True)
        for h in range(HEADS_HERE)
    ]
    sums.append(jnp.zeros((8 - HEADS_HERE, do.shape[0]), FULL))
    delta = jnp.concatenate(sums, axis=0)
    delta_ref[...] = delta
    pack_ref[...] = packed(do, delta)


def self_query_grad(q_ref, kv0, kv1, kv2, kv3, bias_ref, lse_ref, pack_ref, delta_ref, dq_ref):
    q, kv, bias = q_ref[...][:, :WIDE], stacked((kv0, kv1, kv2, kv3)), bias_ref[...]
    do = pack_ref[...]
    rows = []
    for h in range(HEADS_HERE):
        k = head(kv, h)
        p = jnp.exp(nt(k, head(q, h)) * SCALE + bias - lse_ref[h : h + 1, :])
        dp = nt(head(kv, h, WIDE), head(do, h))
        ds = (p * (dp - delta_ref[h : h + 1, :])).astype(LOW)
        rows.append(tn(k, ds) * SCALE)
    dq_ref[...] = jnp.concatenate(rows, axis=0).T.astype(LOW)


def self_key_grad(order_ref, qkv_ref, bias_ref, pack_ref, *refs):
    do_refs, out_ref = refs[:-1], refs[-1]
    kv, bias = qkv_ref[...][:, WIDE:], bias_ref[...]
    count = qkv_ref.shape[0]
    packs = [
        pack_ref[pl.ds(pl.multiple_of(order_ref[d] * count, count), count), :] for d in range(8)
    ]
    lse = jnp.concatenate([stats_of(x) for x in packs], axis=1)
    delta = jnp.concatenate([stats_of(ref[...]) for ref in do_refs], axis=1)
    q, do = jnp.concatenate(packs, axis=0), stacked(do_refs)
    dks, dvs = [], []
    for h in range(HEADS_HERE):
        q_h, do_h = head(q, h), head(do, h)
        p = jnp.exp(nt(head(kv, h), q_h) * SCALE + bias - lse[h : h + 1])
        dp = nt(head(kv, h, WIDE), do_h)
        ds = (p * (dp - delta[h : h + 1])).astype(LOW)
        dks.append(nn(ds, q_h) * SCALE)
        dvs.append(nn(p.astype(LOW), do_h))
    out_ref[...] = jnp.concatenate(dks + dvs, axis=1).astype(LOW)


def cross_backward(
    dy0_ref, dy1_ref, q_ref, kv_ref, bias_ref, lse_ref, w_ref, dq_ref, dkv_ref, out_ref
):
    do = nn(stacked((dy0_ref, dy1_ref)), w_ref[...][:, WIDE:]).astype(LOW)
    dq, dkv = attend_back(do, q_ref[...], kv_ref[...], bias_ref[...], lse_ref)
    dq = dq.astype(LOW)
    dq_ref[...] = dq
    dkv_ref[...] = dkv.astype(LOW)
    out_ref[...] = nt(dq, w_ref[...][:, :WIDE]).astype(LOW)


NORMS = [(l, k) for l in range(2) for k in range(3)]


def norm_sums(*refs):
    out_ref = refs[-1]
    out_ref[...] = jnp.zeros(out_ref.shape, FULL)
    for at in range(len(NORMS)):
        upstream, n = refs[2 * at][...], refs[2 * at + 1][...]
        out_ref[at : at + 1, :] = jnp.sum(upstream * n, axis=0, keepdims=True)
        out_ref[6 + at : 7 + at, :] = jnp.sum(upstream, axis=0, keepdims=True)


def ff_forward(e0_ref, e1_ref, up_ref, down_ref, u_ref, hmid_ref, out_ref):
    u = nn(stacked((e0_ref, e1_ref)), up_ref[...])
    hmid = gelu(u).astype(LOW)
    u_ref[...] = u
    hmid_ref[...] = hmid
    out_ref[...] = nt(hmid, down_ref[...]).astype(LOW)


def ff_backward(dy0_ref, dy1_ref, u_ref, up_ref, down_ref, du_ref, out_ref):
    du = (nn(stacked((dy0_ref, dy1_ref)), down_ref[...]) * gelu_slope(u_ref[...])).astype(LOW)
    du_ref[...] = du
    out_ref[...] = nt(du, up_ref[...]).astype(LOW)


def weight_sums(groups, width):
    steps, args, specs, plan, columns = 4, [], [], [], 0
    rows = width // steps

    def put(x, spec):
        args.append(x)
        specs.append(spec)
        return len(args) - 1

    for group in groups:
        terms = []
        size = 0
        for kind, a, b in group:
            if kind == "tn":
                at = [put(x, lambda x: pl.BlockSpec((x.shape[0], rows), lambda i: (0, i))) for x in a]
                size += b.shape[1]
            else:
                cut, index = a[1]
                at = put(a[0], lambda x, c=cut, k=index: pl.BlockSpec((rows, c), lambda i: (i, k)))
                size = b.shape[0] if kind == "nt" else b.shape[1]
            terms.append((kind, at, put(b, None)))
        plan.append((columns, size, terms))
        columns += size

    def body(*refs):
        out_ref = refs[-1]
        for start, size, terms in plan:
            if terms[0][0] == "tn":
                parts = [tn(stacked([refs[k] for k in a]), refs[b][...]) for _, a, b in terms]
                value = parts[0] if len(parts) == 1 else jnp.concatenate(parts, axis=1)
            else:
                product = nt if terms[0][0] == "nt" else nn
                value = sum(product(refs[a][...], refs[b][...]) for _, a, b in terms)
            out_ref[:, start : start + size] = value.astype(LOW)

    return kernel_call(
        body,
        args,
        [((width, columns), LOW)],
        steps,
        specs,
        [pl.BlockSpec((rows, columns), lambda i: (i, 0))],
        room=24,
    )[0]


def halved(lower, out_refs, columns):
    sides = []
    for side in range(2):
        parts = []
        for x, split in columns:
            size = x.shape[1] // 2
            parts.append(x[:, side * size : (side + 1) * size] if split else x)
        sides.append(jnp.concatenate(parts, axis=1))
    mine, theirs = out_refs

    @pl.when(lower)
    def _():
        mine[...], theirs[...] = sides[0], sides[1]

    @pl.when(jnp.logical_not(lower))
    def _():
        mine[...], theirs[...] = sides[1], sides[0]


def first_columns(here_ref, in_ref, norm_ref, mine, theirs):
    columns = [(in_ref[0, k], True) for k in range(3)] + [(norm_ref[...], False)]
    halved(here_ref[0] == 0, (mine, theirs), columns)


def other_columns(here_ref, in_ref, out_ref, query_ref, text_ref, tout_ref, up_ref, down_ref, memory_ref, *outs):
    lower = here_ref[0] == 0
    spare = jnp.zeros((out_ref.shape[1], WIDE), LOW)

    def text(l):
        pair = [(text_ref[l, k], True) for k in range(2)]
        return pair, [(query_ref[l], True), (tout_ref[l], True)]

    pair, cross = text(0)
    both = [(memory_ref[m], False) for m in range(2)]
    halved(lower, outs[0:2], pair + both + cross + [(out_ref[0], True), (spare, False)])
    feed = [(up_ref[0], True), (down_ref[0], True)]
    pair, cross = text(1)
    own = [(out_ref[1], True)] + [(in_ref[0, k], True) for k in range(3)]
    halved(lower, outs[2:4], feed + pair + cross + own)
    halved(lower, outs[4:6], [(up_ref[1], True), (down_ref[1], True)])


def laid_out(parts, here, strip, ff):
    args = [here.reshape(1)] + [x for pair in parts for x in pair]

    def body(*refs):
        lower = refs[0][0] == 0
        kept = []
        for mine, theirs in ((1, 2), (3, 4), (5, 6)):
            a, b = refs[mine][...].astype(FULL), refs[theirs][...].astype(FULL)
            kept.append((jnp.where(lower, a, b), jnp.where(lower, b, a)))
        early, second, last = kept
        g_in, g_out, g_query, g_text, g_tout, g_up, g_down = refs[7:]

        def wide(pair, start, size):
            return jnp.concatenate([x[:, start : start + size] for x in pair], axis=1)

        for k in range(3):
            g_in[0, k] = wide(last, k * WIDE, WIDE)
            g_in[1, k] = wide(second, 2 * ff + k * WIDE, WIDE)
        g_out[0] = wide(last, 576, WIDE)
        g_out[1] = wide(second, 2 * ff + 576, WIDE)
        for l, pair in enumerate((second, early)):
            g_up[l] = wide(pair, 0, ff)
            g_down[l] = wide(pair, ff, ff)
        for l, (pair, start, next_start) in enumerate(
            ((second, 2304, 2688), (early, 2 * ff, 2 * ff + 384))
        ):
            for k in range(2):
                g_text[l, k] = wide(pair, start + k * WIDE, WIDE)
            g_query[l] = wide(pair, next_start, WIDE)
            g_tout[l] = wide(pair, next_start + WIDE, WIDE)

    outs = [
        ((2, 3, strip, 2 * WIDE), FULL),
        ((2, strip, 2 * WIDE), FULL),
        ((2, strip, 2 * WIDE), FULL),
        ((2, 2, strip, 2 * WIDE), FULL),
        ((2, strip, 2 * WIDE), FULL),
        ((2, strip, 2 * ff), FULL),
        ((2, strip, 2 * ff), FULL),
    ]
    specs = [lambda x: pl.BlockSpec(memory_space=pltpu.SMEM)] + [None] * 6
    return kernel_call(body, args, outs, 1, specs, room=24)


def gelu(z):
    return 0.5 * z * (1.0 + lax.erf(z * math.sqrt(0.5)))


def gelu_slope(z):
    half = 0.5 * (1.0 + lax.erf(z * math.sqrt(0.5)))
    return half + z * jnp.exp(-0.5 * z * z) * (1.0 / math.sqrt(2.0 * math.pi))


def width_mixed(x):
    lead = x.shape[:-1]
    parts = x.reshape(*lead, 8, 4, -1)
    return jnp.swapaxes(parts, -2, -3).reshape(*lead, -1)


def width_restored(x):
    lead = x.shape[:-1]
    parts = x.reshape(*lead, 4, 8, -1)
    return jnp.swapaxes(parts, -2, -3).reshape(*lead, -1)


def local(
    tokens,
    memory,
    clip_lengths,
    out_grad,
    norm_gain,
    norm_bias,
    self_in,
    self_out,
    text_query,
    text_kv,
    text_out,
    mlp_up,
    mlp_down,
):
    xh, core, zh = lax.axis_index("xh"), lax.axis_index("core"), lax.axis_index("zh")
    zl, xl, y = lax.axis_index("zl"), lax.axis_index("xl"), lax.axis_index("y")
    row = xh * 2 + core
    width = tokens.shape[2]
    strip = memory.shape[2]
    ff = mlp_up.shape[2] // 2

    def spread_pair(pair):
        mine, theirs = pair
        theirs = swapped(theirs, "xl")
        return jnp.where(
            xl == 0, jnp.concatenate([mine, theirs]), jnp.concatenate([theirs, mine])
        )

    def spread(both):
        return lax.all_gather(both, SPREAD, axis=0, tiled=True)

    def columns(body, args, sizes, layer):
        scalar = lambda x: pl.BlockSpec(memory_space=pltpu.SMEM)
        one = lambda x: pl.BlockSpec((1, *x.shape[1:]), lambda i: (layer, 0, 0, 0))
        outs = [((strip, size), LOW) for size in sizes for _ in range(2)]
        specs = [scalar, one] + [None] * (len(args) - 1)
        done = kernel_call(body, [xl.reshape(1), *args], outs, specs=specs)
        return [done[k : k + 2] for k in range(0, len(done), 2)]

    norms = jnp.concatenate([norm_gain.reshape(6, strip), norm_bias.reshape(6, strip)])
    norms = jnp.pad(norms.T, ((0, 0), (0, 52)))
    turned = [jnp.swapaxes(x, 1, 2) for x in (self_out, text_out, mlp_down, memory)]

    own_0 = columns(first_columns, [self_in, norms], [640], 0)[0]
    *own_0, tokens, out_grad = tied(*own_0, tokens, out_grad)
    own_0 = spread_pair(own_0)
    here = jnp.concatenate([tokens, out_grad], axis=2)
    here = lax.dynamic_slice_in_dim(here, row * 16, 16, axis=1)
    keep = jnp.where(zh == 0, here[0], here[1])
    send = jnp.where(zh == 0, here[1], here[0])
    own_rows = jnp.concatenate([keep, swapped(send, "zh")], axis=0)
    token_rows = width_mixed(own_rows[:, :width])
    grad_rows = width_mixed(own_rows[:, width:])

    own_0, token_rows, norm_free = tied(own_0, token_rows, turned[0])
    piece_0, token_all = tied(strips_of_all(own_0), jnp.concatenate(rows_of_all(token_rows)))
    pairs = columns(
        other_columns,
        [self_in, norm_free, text_query, text_kv, turned[1], mlp_up, turned[2], turned[3]],
        [1536, 2 * ff + 1536, 2 * ff],
        1,
    )
    piece_1 = spread(spread_pair(pairs[0]))
    piece_2 = spread(spread_pair(pairs[1]))
    w_in_0 = piece_0[:, :576]
    norm_rows = nt(jnp.eye(64, dtype=LOW)[:16], piece_0[:, 576:640])
    gains = [norm_rows[0:3], norm_rows[3:6]]
    shifts = [norm_rows[6:9], norm_rows[9:12]]
    unit_all, _ = unit(token_all.astype(FULL))
    first_normed = (unit_all * gains[0][0] + shifts[0][0]).astype(LOW)
    first_qkv = nn(first_normed, w_in_0).astype(LOW)
    first_normed = [first_normed]
    first_pair = keys_pair(first_qkv[:, WIDE:])
    w_in = [w_in_0, piece_2[:, 2496:]]
    attn, feed = [piece_1, piece_2], [piece_2]
    w_text = [piece_1[:, :384], piece_2[:, 1536:1920]]
    out_window = [window(384, 3), window(384, 6)]
    memory_all = piece_1[:, 384:768]
    up_window, down_window = window(ff, 0), window(ff, 1)
    cross_window = [window(384, 2), window(384, 5)]

    at = jnp.arange(2048, dtype=jnp.int32)
    d_y, d_z, d_c = at // 512, (at // 256) % 2, (at // 128) % 2
    d_x, d_s, inner = (at // 32) % 4, (at // 16) % 2, at % 16
    block = (zh ^ d_s) * 16 + (zl ^ d_z) * 8 + (xl ^ (d_x & 1)) * 4 + (y ^ d_y)
    key_at = block * 64 + ((xh ^ (d_x >> 1)) * 2 + (core ^ d_c)) * 16 + inner
    lengths = jnp.where(zh == 0, clip_lengths[0], clip_lengths[1])
    end_0 = lengths[0]
    end_1 = lengths[0] + lengths[1]
    key_clip = (key_at >= end_0).astype(jnp.int32) + (key_at >= end_1).astype(jnp.int32)
    frame_at, frame_clip = key_at[:256], key_clip[:256]
    allowed = (frame_clip[None, :] == key_clip[:, None]) & (key_at[:, None] <= frame_at[None, :])
    bias = jnp.where(allowed, 0.0, NEG_FILL).astype(FULL)
    back = (key_clip[None, :] == frame_clip[:, None]) & (frame_at[:, None] <= key_at[None, :])
    back_bias = jnp.where(back, 0.0, NEG_FILL).astype(FULL)
    d_block = jnp.arange(8, dtype=jnp.int32)
    keyed_order = (zl ^ (d_block % 2)) * 4 + (y ^ (d_block // 2))
    text_clip = jnp.arange(192, dtype=jnp.int32) // 64
    text_bias = jnp.where(frame_clip[None, :] == text_clip[:, None], 0.0, NEG_FILL).astype(FULL)
    frames = bias.shape[1]
    low_frames = ((frames, WIDE), LOW)
    lse_rows = ((8, frames), FULL)
    partial_rows = ((frames, width), LOW)
    pack_rows = ((frames, 256), LOW)
    packs = []

    residual = token_rows.astype(FULL)
    kept = []
    for l in range(2):
        n_0, r_0 = unit(residual)
        if l == 0:
            a, qkv, pair = first_normed, first_qkv, first_pair
        else:
            a = rows_of_all((n_0 * gains[l][0] + shifts[l][0]).astype(LOW))
            qkv = kernel_call(
                project,
                [*a, attn[l]],
                [((frames, 3 * WIDE), LOW)],
                specs=[None, None, window(768, 3)],
            )[0]
            pair = keys_pair(qkv[:, WIDE:])
        kv = keys_of_all(pair)
        o, lse, pack, part = kernel_call(
            self_forward,
            [qkv, *kv, bias, attn[l]],
            [low_frames, lse_rows, pack_rows, partial_rows],
            specs=[None] * 6 + [out_window[l]],
            room=24,
        )
        if l == 0:
            part, *rest = tied(part, *pairs[2])
            feed_strips = spread_pair(rest)
        else:
            part, feed_strips = tied(part, feed_strips)
            feed.append(spread(feed_strips))
        packs.append(pack)
        x1 = residual + sum_to_rows(part)
        n_1, r_1 = unit(x1)
        c = rows_of_all((n_1 * gains[l][1] + shifts[l][1]).astype(LOW))
        mkv = tn(memory_all, w_text[l]).astype(LOW)
        mkv = jnp.where(zh == 0, mkv[:192], mkv[192:])
        cq, co, clse, part = kernel_call(
            cross_forward,
            [*c, mkv, text_bias, attn[l]],
            [low_frames, low_frames, lse_rows, partial_rows],
            specs=[None] * 4 + [cross_window[l]],
        )
        x2 = x1 + sum_to_rows(part)
        n_2, r_2 = unit(x2)
        e = rows_of_all((n_2 * gains[l][2] + shifts[l][2]).astype(LOW))
        u, hmid, part = kernel_call(
            ff_forward,
            [*e, feed[l], feed[l]],
            [((frames, ff), FULL), ((frames, ff), LOW), partial_rows],
            specs=[None, None, up_window, down_window],
        )
        residual = x2 + sum_to_rows(part)
        kept.append((n_0, r_0, a, qkv, kv, o, lse, n_1, r_1, c, cq, mkv, co, clse, n_2, r_2, e, u, hmid))

    def frames_back(rows):
        pair = rows.reshape(2, 16, -1)
        other = swapped(pair[1], "zh")
        mbs = jnp.where(zh == 0, jnp.stack([pair[0], other]), jnp.stack([other, pair[0]]))
        both = jnp.stack([mbs, swapped(mbs, "core")])
        both = jnp.where(core == 0, both, both[::-1])
        four = jnp.stack([both, swapped(both, "xh")])
        four = jnp.where(xh == 0, four, four[::-1])
        return jnp.moveaxis(four.reshape(4, 2, 16, -1), 0, 1).reshape(2, 64, -1)

    packs = lax.all_gather(jnp.concatenate(packs, axis=1), KEYED, axis=0, tiled=True)
    grad = grad_rows.astype(FULL)
    norm_terms = {}

    def norm_step(l, k, grad, upstream, n, r):
        norm_terms[l, k] = (upstream, n)
        return grad + unit_back(upstream, n, r, gains[l][k])

    def summed(both):
        return lax.psum_scatter(both, SPREAD, scatter_dimension=0, tiled=True)

    memory_terms = []
    for l in (1, 0):
        n_0, r_0, a, qkv, kv, o, lse, n_1, r_1, c, cq, mkv, co, clse, n_2, r_2, e, u, hmid = kept[l]
        dy = rows_of_all(grad.astype(LOW))
        du, part = kernel_call(
            ff_backward,
            [*dy, u, feed[l], feed[l]],
            [((frames, ff), LOW), partial_rows],
            specs=[None] * 3 + [up_window, down_window],
        )
        de = sum_to_rows(part)
        groups = [[("tn", e, du)], [("tn", dy, hmid)]]
        grad = norm_step(l, 2, grad, de, n_2, r_2)

        dy = rows_of_all(grad.astype(LOW))
        dcq, dmkv, part = kernel_call(
            cross_backward,
            [*dy, cq, mkv, text_bias, clse, attn[l]],
            [low_frames, ((192, 2 * WIDE), LOW), partial_rows],
            specs=[None] * 6 + [cross_window[l]],
        )
        if l == 1:
            part, packs = tied(part, packs)
        dc = sum_to_rows(part)
        none = jnp.zeros_like(dmkv)
        dmkv = jnp.where(
            zh == 0, jnp.concatenate([dmkv, none]), jnp.concatenate([none, dmkv])
        )
        memory_terms.append(("nt", (attn[l], (384, 4 * l)), dmkv))
        cross = [[("nn", (piece_1, (384, 1)), dmkv)], [("tn", c, dcq), ("tn", dy, co)]]
        if l == 1:
            early = weight_sums(groups + cross, width)
            dc, early = tied(dc, early)
            early = summed(early)
        else:
            second = weight_sums(groups + late + cross + [memory_terms], width)
            dc, second, early = tied(dc, second, early)
            second = summed(second)
        grad = norm_step(l, 1, grad, dc, n_1, r_1)

        dy = rows_of_all(grad.astype(LOW))
        do_pack, delta = kernel_call(
            self_upstream,
            [*dy, o, attn[l]],
            [pack_rows, lse_rows],
            specs=[None] * 3 + [out_window[l]],
        )
        do_packs = keyed_of_all(do_pack)
        dq = kernel_call(
            self_query_grad,
            [qkv, *kv, bias, lse, do_pack, delta],
            [low_frames],
            room=32,
        )[0]
        dkv = kernel_call(
            self_key_grad,
            [keyed_order, qkv, back_bias, packs, *do_packs],
            [((frames, 2 * WIDE), LOW)],
            specs=[lambda x: pl.BlockSpec(memory_space=pltpu.SMEM), None, None, window(256, l)]
            + [None] * 8,
            room=32,
        )[0]
        dqkv = jnp.concatenate([dq, dkv], axis=1)
        da = nt(dqkv, w_in[l])
        late = [[("tn", a, dqkv), ("tn", dy, o)]]
        if l == 1:
            grad = norm_step(l, 0, grad, sum_to_rows(da), n_0, r_0)
        else:
            norm_terms[0, 0] = (da, unit_all)
            last = weight_sums(late, width)
            sums = kernel_call(
                norm_sums,
                [x for l, k in NORMS for x in norm_terms[l, k]],
                [((16, width), FULL)],
            )[0]
            extra = jnp.broadcast_to(sums[None], (8, *sums.shape))
            da = jnp.concatenate([da.reshape(8, -1, width), extra], axis=1)
            da = sum_to_rows(da.reshape(-1, width))
            da, last = tied(da, last)
            last = strip_of(sum_along(sum_along(strip_blocks(last), "y"), DEEP))
            norm_total = da[-16:].astype(LOW).reshape(16, 16, -1)
            norm_total = lax.all_to_all(jnp.swapaxes(norm_total, 0, 1), SPREAD, 0, 0, tiled=True)
            norm_total = jnp.sum(norm_total.astype(FULL), axis=0)
            grad = grad + unit_back(da[:-16], n_0, r_0, gains[0][0])
    ends = jnp.concatenate(
        [width_restored(residual.astype(LOW)), width_restored(grad.astype(LOW))], axis=1
    )
    ends = frames_back(ends)
    output, input_grad = ends[:, :, :width], ends[:, :, width:].astype(FULL)

    def strips(block):
        mine = lax.dynamic_slice_in_dim(block, xl * strip, strip, axis=0)
        theirs = lax.dynamic_slice_in_dim(block, (1 - xl) * strip, strip, axis=0)
        return mine, swapped(theirs, "xl")

    def both(pair, start, size):
        return sum(x[:, start : start + size].astype(FULL) for x in pair)

    def everywhere(x):
        x = x + swapped(x.astype(LOW), "core").astype(FULL)
        return x + swapped(x.astype(LOW), "xh").astype(FULL)

    early, second, last = [strips(b) for b in (early, second, last)]
    laid = laid_out((early, second, last), xl, strip, ff)
    self_in_grad, self_out_grad, text_query_grad, text_kv_grad = laid[:4]
    text_out_grad, mlp_up_grad, mlp_down_grad = laid[4:]
    self_out_grad, text_out_grad, mlp_down_grad = [
        jnp.swapaxes(x, 1, 2) for x in (self_out_grad, text_out_grad, mlp_down_grad)
    ]
    memory_grad = everywhere(both(second, 3072, 384)).reshape(strip, 2, 192)
    memory_grad = jnp.transpose(memory_grad, (1, 2, 0))
    norm_grads = lax.dynamic_slice_in_dim(norm_total, xl * strip, strip, axis=1)
    gain_grad = norm_grads[:6].reshape(2, 3, strip)
    shift_grad = norm_grads[6:12].reshape(2, 3, strip)
    return (
        output,
        input_grad,
        memory_grad,
        gain_grad,
        shift_grad[:, 0:2],
        shift_grad[:, 2],
        self_in_grad,
        self_out_grad,
        text_query_grad,
        text_kv_grad,
        text_out_grad,
        mlp_up_grad,
        mlp_down_grad,
    )


def solution(mesh):
    fine = Mesh(mesh.devices.reshape(FINE_SIZES), FINE)
    frames = P(None, COL, None)
    strips = P(None, None, COL)
    return jax.shard_map(
        local,
        mesh=fine,
        in_specs=(
            frames,
            strips,
            P(),
            frames,
            strips,
            strips,
            P(None, None, COL, ROW),
            P(None, ROW, COL),
            P(None, COL, ROW),
            P(None, None, COL, ROW),
            P(None, ROW, COL),
            P(None, COL, ROW),
            P(None, ROW, COL),
        ),
        out_specs=(
            frames,
            frames,
            strips,
            strips,
            strips,
            P(None, COL),
            P(None, None, COL, ROW),
            P(None, ROW, COL),
            P(None, COL, ROW),
            P(None, None, COL, ROW),
            P(None, ROW, COL),
            P(None, COL, ROW),
            P(None, ROW, COL),
        ),
        check_vma=False,
    )
```

```python
import math

import jax
import jax.numpy as jnp
from jax import lax
from jax.experimental import pallas as pl
from jax.experimental.pallas import tpu as pltpu
from jax.sharding import Mesh, PartitionSpec as P

HEAD = 64
HEADS_HERE = 3
WIDE = HEAD * HEADS_HERE
NEG_FILL = -1e30
NORM_EPS = 1e-05
SCALE = 1.0 / math.sqrt(HEAD)
LOW = jnp.bfloat16
FULL = jnp.float32

FINE = ("xh", "core", "zh", "zl", "xl", "y")
FINE_SIZES = (2, 2, 2, 2, 2, 4)
ROW = ("xh", "core")
COL = ("zh", "zl", "xl", "y")
CHIPS = ("xh", "xl")
SPREAD = ("y", "zh", "zl")
DEEP = ("zh", "zl")
KEYED = ("zl", "y")
SWAP = ((0, 1), (1, 0))


def flipped(size, mask):
    return [(i, i ^ mask) for i in range(size)]


def swapped(x, axis):
    return lax.ppermute(x, axis, SWAP)


def rows_of_all(rows):
    chips = [rows] + [lax.ppermute(rows, CHIPS, flipped(4, d)) for d in (1, 2, 3)]
    half = jnp.concatenate(chips, axis=0)
    return [half, swapped(half, "core")]


def sum_to_rows(partial):
    count = partial.shape[0] // 8
    blocks = partial.reshape(2, 4, count, partial.shape[1])
    both = blocks[0].astype(FULL) + swapped(blocks[1].astype(LOW), "core").astype(FULL)
    low = both.astype(LOW)
    total = both[0]
    for d in (1, 2, 3):
        total = total + lax.ppermute(low[d], CHIPS, flipped(4, d)).astype(FULL)
    return total


def keys_pair(block):
    return jnp.concatenate([block, swapped(block, "zl")], axis=0)


def keys_of_all(pair):
    return [pair] + [lax.ppermute(pair, "y", flipped(4, d)) for d in (1, 2, 3)]


def keyed_mask(d):
    return (d & 1) * 4 + d // 2


def keyed_of_all(block):
    return [block] + [
        lax.ppermute(block, KEYED, flipped(8, keyed_mask(d))) for d in range(1, 8)
    ]


def strips_of_all(own):
    y = lax.axis_index("y")
    z = lax.axis_index("zh") * 2 + lax.axis_index("zl")
    places = {"y": (0, y), DEEP: (1, z)}
    rows = own.shape[0] // 2

    def level(x, axis):
        at, here = places[axis]
        shape = list(x.shape)
        shape[at] = 4
        out = jnp.zeros(shape, x.dtype)
        out = lax.dynamic_update_slice_in_dim(out, x, here, axis=at)
        for d in (1, 3, 2):
            part = lax.ppermute(x, axis, flipped(4, d))
            out = lax.dynamic_update_slice_in_dim(out, part, here ^ d, axis=at)
        return out

    halves = own.reshape(1, 1, 2, rows, -1)
    first = level(level(halves[:, :, 0], DEEP), "y")
    second = level(level(halves[:, :, 1], "y"), DEEP)
    return jnp.stack([first, second], axis=2).reshape(32 * rows, -1)


def strip_blocks(partial):
    return partial.reshape(4, 4, partial.shape[0] // 16, -1)


def sum_along(values, axis):
    if axis == "y":
        at, here = 0, lax.axis_index("y")
    else:
        at, here = 1, lax.axis_index("zh") * 2 + lax.axis_index("zl")
    low = values.astype(LOW)

    def block(x, d):
        return lax.dynamic_slice_in_dim(x, here ^ d, 1, axis=at)

    total = block(values, 0).astype(FULL)
    for d in (1, 3, 2):
        total = total + lax.ppermute(block(low, d), axis, flipped(4, d)).astype(FULL)
    return total


def strip_of(total):
    return total.reshape(-1, total.shape[-1]).astype(LOW)


def tied(*arrays):
    return lax.optimization_barrier(arrays)


def mm(a, b, dims):
    return lax.dot_general(a, b, (dims, ((), ())), preferred_element_type=FULL)


def nn(a, b):
    return mm(a, b, ((1,), (0,)))


def nt(a, b):
    return mm(a, b, ((1,), (1,)))


def tn(a, b):
    return mm(a, b, ((0,), (0,)))


def unit(values):
    centre = jnp.mean(values, axis=-1, keepdims=True)
    centred = values - centre
    inverse = lax.rsqrt(jnp.mean(centred * centred, axis=-1, keepdims=True) + NORM_EPS)
    return centred * inverse, inverse


def unit_back(upstream, unit_rows, inverse, gain_row):
    scaled = upstream * gain_row
    inner = (
        scaled
        - jnp.mean(scaled, axis=-1, keepdims=True)
        - unit_rows * jnp.mean(scaled * unit_rows, axis=-1, keepdims=True)
    )
    return inner * inverse


def whole(x):
    return pl.BlockSpec(x.shape, lambda i: (0,) * x.ndim)


def window(columns, index, rows=None):
    return lambda x: pl.BlockSpec((x.shape[0], columns), lambda i: (0, index))


def kernel_call(body, args, outs, steps=1, specs=None, out_specs=None, room=16):
    shapes = [jax.ShapeDtypeStruct(shape, kind) for shape, kind in outs]
    placed = [(spec or whole)(x) for x, spec in zip(args, specs or [None] * len(args))]
    return pl.pallas_call(
        body,
        grid=(steps,),
        in_specs=placed,
        out_specs=out_specs or [whole(x) for x in shapes],
        out_shape=shapes,
        compiler_params=pltpu.CompilerParams(vmem_limit_bytes=room * 2**20),
    )(*args)


def stacked(refs):
    return jnp.concatenate([ref[...] for ref in refs], axis=0)


def head(x, h, start=0):
    return x[:, start + h * HEAD : start + (h + 1) * HEAD]


def attend_into(q, kv, bias, o_ref, lse_ref):
    rows = []
    for h in range(HEADS_HERE):
        s = nt(head(kv, h), head(q, h)) * SCALE + bias
        top = jnp.max(s, axis=0, keepdims=True)
        lse = top + jnp.log(jnp.sum(jnp.exp(s - top), axis=0, keepdims=True))
        p = jnp.exp(s - lse).astype(LOW)
        lse_ref[h : h + 1, :] = lse
        rows.append(tn(head(kv, h, WIDE), p))
    lse_ref[HEADS_HERE:, :] = jnp.zeros((8 - HEADS_HERE, lse_ref.shape[1]), FULL)
    o = jnp.concatenate(rows, axis=0).T.astype(LOW)
    o_ref[...] = o
    return o


def packed(values, stats):
    columns = stats.T
    high = columns.astype(LOW)
    rest = columns - high.astype(FULL)
    middle = rest.astype(LOW)
    low = (rest - middle.astype(FULL)).astype(LOW)
    spare = jnp.zeros((values.shape[0], 256 - values.shape[1] - 3 * 8), LOW)
    return jnp.concatenate([values, high, middle, low, spare], axis=1)


def stats_of(pack):
    turned = pack[:, 128:256].astype(FULL).T
    return turned[64:72] + turned[72:80] + turned[80:88]


def attend_back(do, q, kv, bias, lse_ref):
    dqs, dks, dvs = [], [], []
    for h in range(HEADS_HERE):
        k, v, q_h, do_h = head(kv, h), head(kv, h, WIDE), head(q, h), head(do, h)
        p = jnp.exp(nt(k, q_h) * SCALE + bias - lse_ref[h : h + 1, :])
        dp = nt(v, do_h)
        inner = jnp.sum(p * dp, axis=0, keepdims=True)
        ds = (p * (dp - inner)).astype(LOW)
        dqs.append(tn(k, ds) * SCALE)
        dks.append(nn(ds, q_h) * SCALE)
        dvs.append(nn(p.astype(LOW), do_h))
    dq = jnp.concatenate(dqs, axis=0).T
    return dq, jnp.concatenate(dks + dvs, axis=1)


def project(a0_ref, a1_ref, w_ref, out_ref):
    out_ref[...] = nn(stacked((a0_ref, a1_ref)), w_ref[...][:, WIDE:]).astype(LOW)


def self_forward(q_ref, kv0, kv1, kv2, kv3, bias_ref, w_ref, o_ref, lse_ref, pack_ref, out_ref):
    q = q_ref[...][:, :WIDE]
    o = attend_into(q, stacked((kv0, kv1, kv2, kv3)), bias_ref[...], o_ref, lse_ref)
    pack_ref[...] = packed(q, lse_ref[...])
    out_ref[...] = nt(o, w_ref[...][:, :WIDE]).astype(LOW)


def cross_forward(c0_ref, c1_ref, kv_ref, bias_ref, w_ref, q_ref, o_ref, lse_ref, out_ref):
    q = nn(stacked((c0_ref, c1_ref)), w_ref[...][:, :WIDE]).astype(LOW)
    q_ref[...] = q
    o = attend_into(q, kv_ref[...], bias_ref[...], o_ref, lse_ref)
    out_ref[...] = nt(o, w_ref[...][:, WIDE:]).astype(LOW)


def self_upstream(dy0_ref, dy1_ref, o_ref, w_ref, pack_ref, delta_ref):
    do = nn(stacked((dy0_ref, dy1_ref)), w_ref[...][:, :WIDE]).astype(LOW)
    product = (do.astype(FULL) * o_ref[...].astype(FULL)).T
    sums = [
        jnp.sum(product[h * HEAD : (h + 1) * HEAD], axis=0, keepdims=True)
        for h in range(HEADS_HERE)
    ]
    sums.append(jnp.zeros((8 - HEADS_HERE, do.shape[0]), FULL))
    delta = jnp.concatenate(sums, axis=0)
    delta_ref[...] = delta
    pack_ref[...] = packed(do, delta)


def self_query_grad(q_ref, kv0, kv1, kv2, kv3, bias_ref, lse_ref, pack_ref, delta_ref, dq_ref):
    q, kv, bias = q_ref[...][:, :WIDE], stacked((kv0, kv1, kv2, kv3)), bias_ref[...]
    do = pack_ref[...]
    rows = []
    for h in range(HEADS_HERE):
        k = head(kv, h)
        p = jnp.exp(nt(k, head(q, h)) * SCALE + bias - lse_ref[h : h + 1, :])
        dp = nt(head(kv, h, WIDE), head(do, h))
        ds = (p * (dp - delta_ref[h : h + 1, :])).astype(LOW)
        rows.append(tn(k, ds) * SCALE)
    dq_ref[...] = jnp.concatenate(rows, axis=0).T.astype(LOW)


def self_key_grad(order_ref, qkv_ref, bias_ref, pack_ref, *refs):
    do_refs, out_ref = refs[:-1], refs[-1]
    kv, bias = qkv_ref[...][:, WIDE:], bias_ref[...]
    count = qkv_ref.shape[0]
    packs = [
        pack_ref[pl.ds(pl.multiple_of(order_ref[d] * count, count), count), :] for d in range(8)
    ]
    lse = jnp.concatenate([stats_of(x) for x in packs], axis=1)
    delta = jnp.concatenate([stats_of(ref[...]) for ref in do_refs], axis=1)
    q, do = jnp.concatenate(packs, axis=0), stacked(do_refs)
    dks, dvs = [], []
    for h in range(HEADS_HERE):
        q_h, do_h = head(q, h), head(do, h)
        p = jnp.exp(nt(head(kv, h), q_h) * SCALE + bias - lse[h : h + 1])
        dp = nt(head(kv, h, WIDE), do_h)
        ds = (p * (dp - delta[h : h + 1])).astype(LOW)
        dks.append(nn(ds, q_h) * SCALE)
        dvs.append(nn(p.astype(LOW), do_h))
    out_ref[...] = jnp.concatenate(dks + dvs, axis=1).astype(LOW)


def cross_backward(
    dy0_ref, dy1_ref, q_ref, kv_ref, bias_ref, lse_ref, w_ref, dq_ref, dkv_ref, out_ref
):
    do = nn(stacked((dy0_ref, dy1_ref)), w_ref[...][:, WIDE:]).astype(LOW)
    dq, dkv = attend_back(do, q_ref[...], kv_ref[...], bias_ref[...], lse_ref)
    dq = dq.astype(LOW)
    dq_ref[...] = dq
    dkv_ref[...] = dkv.astype(LOW)
    out_ref[...] = nt(dq, w_ref[...][:, :WIDE]).astype(LOW)


NORMS = [(l, k) for l in range(2) for k in range(3)]


def norm_sums(*refs):
    out_ref = refs[-1]
    out_ref[...] = jnp.zeros(out_ref.shape, FULL)
    for at in range(len(NORMS)):
        upstream, n = refs[2 * at][...], refs[2 * at + 1][...]
        out_ref[at : at + 1, :] = jnp.sum(upstream * n, axis=0, keepdims=True)
        out_ref[6 + at : 7 + at, :] = jnp.sum(upstream, axis=0, keepdims=True)


def ff_forward(e0_ref, e1_ref, up_ref, down_ref, u_ref, hmid_ref, out_ref):
    u = nn(stacked((e0_ref, e1_ref)), up_ref[...])
    hmid = gelu(u).astype(LOW)
    u_ref[...] = u
    hmid_ref[...] = hmid
    out_ref[...] = nt(hmid, down_ref[...]).astype(LOW)


def ff_backward(dy0_ref, dy1_ref, u_ref, up_ref, down_ref, du_ref, out_ref):
    du = (nn(stacked((dy0_ref, dy1_ref)), down_ref[...]) * gelu_slope(u_ref[...])).astype(LOW)
    du_ref[...] = du
    out_ref[...] = nt(du, up_ref[...]).astype(LOW)


def weight_sums(groups, width):
    steps, args, specs, plan, columns = 4, [], [], [], 0
    rows = width // steps

    def put(x, spec):
        args.append(x)
        specs.append(spec)
        return len(args) - 1

    for group in groups:
        terms = []
        size = 0
        for kind, a, b in group:
            if kind == "tn":
                at = [put(x, lambda x: pl.BlockSpec((x.shape[0], rows), lambda i: (0, i))) for x in a]
                size += b.shape[1]
            else:
                cut, index = a[1]
                at = put(a[0], lambda x, c=cut, k=index: pl.BlockSpec((rows, c), lambda i: (i, k)))
                size = b.shape[0] if kind == "nt" else b.shape[1]
            terms.append((kind, at, put(b, None)))
        plan.append((columns, size, terms))
        columns += size

    def body(*refs):
        out_ref = refs[-1]
        for start, size, terms in plan:
            if terms[0][0] == "tn":
                parts = [tn(stacked([refs[k] for k in a]), refs[b][...]) for _, a, b in terms]
                value = parts[0] if len(parts) == 1 else jnp.concatenate(parts, axis=1)
            else:
                product = nt if terms[0][0] == "nt" else nn
                value = sum(product(refs[a][...], refs[b][...]) for _, a, b in terms)
            out_ref[:, start : start + size] = value.astype(LOW)

    return kernel_call(
        body,
        args,
        [((width, columns), LOW)],
        steps,
        specs,
        [pl.BlockSpec((rows, columns), lambda i: (i, 0))],
        room=24,
    )[0]


def halved(lower, out_refs, columns):
    sides = []
    for side in range(2):
        parts = []
        for x, split in columns:
            size = x.shape[1] // 2
            parts.append(x[:, side * size : (side + 1) * size] if split else x)
        sides.append(jnp.concatenate(parts, axis=1))
    mine, theirs = out_refs

    @pl.when(lower)
    def _():
        mine[...], theirs[...] = sides[0], sides[1]

    @pl.when(jnp.logical_not(lower))
    def _():
        mine[...], theirs[...] = sides[1], sides[0]


def first_columns(here_ref, in_ref, norm_ref, mine, theirs):
    columns = [(in_ref[0, k], True) for k in range(3)] + [(norm_ref[...], False)]
    halved(here_ref[0] == 0, (mine, theirs), columns)


def other_columns(here_ref, in_ref, out_ref, query_ref, text_ref, tout_ref, up_ref, down_ref, memory_ref, *outs):
    lower = here_ref[0] == 0
    spare = jnp.zeros((out_ref.shape[1], WIDE), LOW)

    def text(l):
        pair = [(text_ref[l, k], True) for k in range(2)]
        return pair, [(query_ref[l], True), (tout_ref[l], True)]

    pair, cross = text(0)
    both = [(memory_ref[m], False) for m in range(2)]
    halved(lower, outs[0:2], pair + both + cross + [(out_ref[0], True), (spare, False)])
    feed = [(up_ref[0], True), (down_ref[0], True)]
    pair, cross = text(1)
    own = [(out_ref[1], True)] + [(in_ref[0, k], True) for k in range(3)]
    halved(lower, outs[2:4], feed + pair + cross + own)
    halved(lower, outs[4:6], [(up_ref[1], True), (down_ref[1], True)])


def laid_out(parts, here, strip, ff):
    args = [here.reshape(1)] + [x for pair in parts for x in pair]

    def body(*refs):
        lower = refs[0][0] == 0
        kept = []
        for mine, theirs in ((1, 2), (3, 4), (5, 6)):
            a, b = refs[mine][...].astype(FULL), refs[theirs][...].astype(FULL)
            kept.append((jnp.where(lower, a, b), jnp.where(lower, b, a)))
        early, second, last = kept
        g_in, g_out, g_query, g_text, g_tout, g_up, g_down = refs[7:]

        def wide(pair, start, size):
            return jnp.concatenate([x[:, start : start + size] for x in pair], axis=1)

        for k in range(3):
            g_in[0, k] = wide(last, k * WIDE, WIDE)
            g_in[1, k] = wide(second, 2 * ff + k * WIDE, WIDE)
        g_out[0] = wide(last, 576, WIDE)
        g_out[1] = wide(second, 2 * ff + 576, WIDE)
        for l, pair in enumerate((second, early)):
            g_up[l] = wide(pair, 0, ff)
            g_down[l] = wide(pair, ff, ff)
        for l, (pair, start, next_start) in enumerate(
            ((second, 2304, 2688), (early, 2 * ff, 2 * ff + 384))
        ):
            for k in range(2):
                g_text[l, k] = wide(pair, start + k * WIDE, WIDE)
            g_query[l] = wide(pair, next_start, WIDE)
            g_tout[l] = wide(pair, next_start + WIDE, WIDE)

    outs = [
        ((2, 3, strip, 2 * WIDE), FULL),
        ((2, strip, 2 * WIDE), FULL),
        ((2, strip, 2 * WIDE), FULL),
        ((2, 2, strip, 2 * WIDE), FULL),
        ((2, strip, 2 * WIDE), FULL),
        ((2, strip, 2 * ff), FULL),
        ((2, strip, 2 * ff), FULL),
    ]
    specs = [lambda x: pl.BlockSpec(memory_space=pltpu.SMEM)] + [None] * 6
    return kernel_call(body, args, outs, 1, specs, room=24)


def gelu(z):
    return 0.5 * z * (1.0 + lax.erf(z * math.sqrt(0.5)))


def gelu_slope(z):
    half = 0.5 * (1.0 + lax.erf(z * math.sqrt(0.5)))
    return half + z * jnp.exp(-0.5 * z * z) * (1.0 / math.sqrt(2.0 * math.pi))


def width_mixed(x):
    lead = x.shape[:-1]
    parts = x.reshape(*lead, 8, 4, -1)
    return jnp.swapaxes(parts, -2, -3).reshape(*lead, -1)


def shuffled(x, order):
    size = x.shape[1] // len(order)
    return jnp.concatenate([x[:, k * size : (k + 1) * size] for k in order], axis=1)


def rows_mixed(rows_ref, out_ref):
    order = [(p % 8) * 4 + p // 8 for p in range(32)]
    out_ref[...] = shuffled(rows_ref[...].astype(FULL), order).astype(LOW)


def rows_restored(last_ref, grad_ref, out_ref):
    order = [(c % 4) * 8 + c // 4 for c in range(32)]
    width = last_ref.shape[1]
    out_ref[:, :width] = shuffled(last_ref[...], order).astype(LOW)
    out_ref[:, width:] = shuffled(grad_ref[...], order).astype(LOW)


def local(
    tokens,
    memory,
    clip_lengths,
    out_grad,
    norm_gain,
    norm_bias,
    self_in,
    self_out,
    text_query,
    text_kv,
    text_out,
    mlp_up,
    mlp_down,
):
    xh, core, zh = lax.axis_index("xh"), lax.axis_index("core"), lax.axis_index("zh")
    zl, xl, y = lax.axis_index("zl"), lax.axis_index("xl"), lax.axis_index("y")
    row = xh * 2 + core
    width = tokens.shape[2]
    strip = memory.shape[2]
    ff = mlp_up.shape[2] // 2

    def spread_pair(pair):
        mine, theirs = pair
        theirs = swapped(theirs, "xl")
        return jnp.where(
            xl == 0, jnp.concatenate([mine, theirs]), jnp.concatenate([theirs, mine])
        )

    def spread(both):
        return lax.all_gather(both, SPREAD, axis=0, tiled=True)

    def columns(body, args, sizes, layer):
        scalar = lambda x: pl.BlockSpec(memory_space=pltpu.SMEM)
        one = lambda x: pl.BlockSpec((1, *x.shape[1:]), lambda i: (layer, 0, 0, 0))
        outs = [((strip, size), LOW) for size in sizes for _ in range(2)]
        specs = [scalar, one] + [None] * (len(args) - 1)
        done = kernel_call(body, [xl.reshape(1), *args], outs, specs=specs)
        return [done[k : k + 2] for k in range(0, len(done), 2)]

    norms = jnp.concatenate([norm_gain.reshape(6, strip), norm_bias.reshape(6, strip)])
    norms = jnp.pad(norms.T, ((0, 0), (0, 52)))
    turned = [jnp.swapaxes(x, 1, 2) for x in (self_out, text_out, mlp_down, memory)]

    own_0 = columns(first_columns, [self_in, norms], [640], 0)[0]
    *own_0, tokens, out_grad = tied(*own_0, tokens, out_grad)
    own_0 = spread_pair(own_0)
    here = jnp.concatenate([tokens, out_grad], axis=2)
    here = lax.dynamic_slice_in_dim(here, row * 16, 16, axis=1)
    keep = jnp.where(zh == 0, here[0], here[1])
    send = jnp.where(zh == 0, here[1], here[0])
    own_rows = jnp.concatenate([keep, swapped(send, "zh")], axis=0)
    token_rows = width_mixed(own_rows[:, :width])
    grad_rows = kernel_call(rows_mixed, [own_rows[:, width:]], [((32, width), LOW)])[0]

    own_0, token_rows, norm_free = tied(own_0, token_rows, turned[0])
    piece_0, token_all = tied(strips_of_all(own_0), jnp.concatenate(rows_of_all(token_rows)))
    pairs = columns(
        other_columns,
        [self_in, norm_free, text_query, text_kv, turned[1], mlp_up, turned[2], turned[3]],
        [1536, 2 * ff + 1536, 2 * ff],
        1,
    )
    piece_1 = spread(spread_pair(pairs[0]))
    piece_2 = spread(spread_pair(pairs[1]))
    w_in_0 = piece_0[:, :576]
    norm_rows = nt(jnp.eye(64, dtype=LOW)[:16], piece_0[:, 576:640])
    gains = [norm_rows[0:3], norm_rows[3:6]]
    shifts = [norm_rows[6:9], norm_rows[9:12]]
    unit_all, _ = unit(token_all.astype(FULL))
    first_normed = (unit_all * gains[0][0] + shifts[0][0]).astype(LOW)
    first_qkv = nn(first_normed, w_in_0).astype(LOW)
    first_normed = [first_normed]
    first_pair = keys_pair(first_qkv[:, WIDE:])
    w_in = [w_in_0, piece_2[:, 2496:]]
    attn, feed = [piece_1, piece_2], [piece_2]
    w_text = [piece_1[:, :384], piece_2[:, 1536:1920]]
    out_window = [window(384, 3), window(384, 6)]
    memory_all = piece_1[:, 384:768]
    up_window, down_window = window(ff, 0), window(ff, 1)
    cross_window = [window(384, 2), window(384, 5)]

    at = jnp.arange(2048, dtype=jnp.int32)
    d_y, d_z, d_c = at // 512, (at // 256) % 2, (at // 128) % 2
    d_x, d_s, inner = (at // 32) % 4, (at // 16) % 2, at % 16
    block = (zh ^ d_s) * 16 + (zl ^ d_z) * 8 + (xl ^ (d_x & 1)) * 4 + (y ^ d_y)
    key_at = block * 64 + ((xh ^ (d_x >> 1)) * 2 + (core ^ d_c)) * 16 + inner
    lengths = jnp.where(zh == 0, clip_lengths[0], clip_lengths[1])
    end_0 = lengths[0]
    end_1 = lengths[0] + lengths[1]
    key_clip = (key_at >= end_0).astype(jnp.int32) + (key_at >= end_1).astype(jnp.int32)
    frame_at, frame_clip = key_at[:256], key_clip[:256]
    allowed = (frame_clip[None, :] == key_clip[:, None]) & (key_at[:, None] <= frame_at[None, :])
    bias = jnp.where(allowed, 0.0, NEG_FILL).astype(FULL)
    back = (key_clip[None, :] == frame_clip[:, None]) & (frame_at[:, None] <= key_at[None, :])
    back_bias = jnp.where(back, 0.0, NEG_FILL).astype(FULL)
    d_block = jnp.arange(8, dtype=jnp.int32)
    keyed_order = (zl ^ (d_block % 2)) * 4 + (y ^ (d_block // 2))
    text_clip = jnp.arange(192, dtype=jnp.int32) // 64
    text_bias = jnp.where(frame_clip[None, :] == text_clip[:, None], 0.0, NEG_FILL).astype(FULL)
    frames = bias.shape[1]
    low_frames = ((frames, WIDE), LOW)
    lse_rows = ((8, frames), FULL)
    partial_rows = ((frames, width), LOW)
    pack_rows = ((frames, 256), LOW)
    packs = []

    residual = token_rows.astype(FULL)
    kept = []
    for l in range(2):
        n_0, r_0 = unit(residual)
        if l == 0:
            a, qkv, pair = first_normed, first_qkv, first_pair
        else:
            a = rows_of_all((n_0 * gains[l][0] + shifts[l][0]).astype(LOW))
            qkv = kernel_call(
                project,
                [*a, attn[l]],
                [((frames, 3 * WIDE), LOW)],
                specs=[None, None, window(768, 3)],
            )[0]
            pair = keys_pair(qkv[:, WIDE:])
        kv = keys_of_all(pair)
        o, lse, pack, part = kernel_call(
            self_forward,
            [qkv, *kv, bias, attn[l]],
            [low_frames, lse_rows, pack_rows, partial_rows],
            specs=[None] * 6 + [out_window[l]],
            room=24,
        )
        if l == 0:
            part, *rest = tied(part, *pairs[2])
            feed_strips = spread_pair(rest)
        else:
            part, feed_strips = tied(part, feed_strips)
            feed.append(spread(feed_strips))
        packs.append(pack)
        x1 = residual + sum_to_rows(part)
        n_1, r_1 = unit(x1)
        c = rows_of_all((n_1 * gains[l][1] + shifts[l][1]).astype(LOW))
        mkv = tn(memory_all, w_text[l]).astype(LOW)
        mkv = jnp.where(zh == 0, mkv[:192], mkv[192:])
        cq, co, clse, part = kernel_call(
            cross_forward,
            [*c, mkv, text_bias, attn[l]],
            [low_frames, low_frames, lse_rows, partial_rows],
            specs=[None] * 4 + [cross_window[l]],
        )
        x2 = x1 + sum_to_rows(part)
        n_2, r_2 = unit(x2)
        e = rows_of_all((n_2 * gains[l][2] + shifts[l][2]).astype(LOW))
        u, hmid, part = kernel_call(
            ff_forward,
            [*e, feed[l], feed[l]],
            [((frames, ff), FULL), ((frames, ff), LOW), partial_rows],
            specs=[None, None, up_window, down_window],
        )
        residual = x2 + sum_to_rows(part)
        kept.append((n_0, r_0, a, qkv, kv, o, lse, n_1, r_1, c, cq, mkv, co, clse, n_2, r_2, e, u, hmid))

    def frames_back(rows):
        pair = rows.reshape(2, 16, -1)
        other = swapped(pair[1], "zh")
        mbs = jnp.where(zh == 0, jnp.stack([pair[0], other]), jnp.stack([other, pair[0]]))
        both = jnp.stack([mbs, swapped(mbs, "core")])
        both = jnp.where(core == 0, both, both[::-1])
        four = jnp.stack([both, swapped(both, "xh")])
        four = jnp.where(xh == 0, four, four[::-1])
        return jnp.moveaxis(four.reshape(4, 2, 16, -1), 0, 1).reshape(2, 64, -1)

    packs = lax.all_gather(jnp.concatenate(packs, axis=1), KEYED, axis=0, tiled=True)
    grad = grad_rows.astype(FULL)
    norm_terms = {}

    def norm_step(l, k, grad, upstream, n, r):
        norm_terms[l, k] = (upstream, n)
        return grad + unit_back(upstream, n, r, gains[l][k])

    def summed(both):
        return lax.psum_scatter(both, SPREAD, scatter_dimension=0, tiled=True)

    memory_terms = []
    for l in (1, 0):
        n_0, r_0, a, qkv, kv, o, lse, n_1, r_1, c, cq, mkv, co, clse, n_2, r_2, e, u, hmid = kept[l]
        dy = rows_of_all(grad.astype(LOW))
        du, part = kernel_call(
            ff_backward,
            [*dy, u, feed[l], feed[l]],
            [((frames, ff), LOW), partial_rows],
            specs=[None] * 3 + [up_window, down_window],
        )
        de = sum_to_rows(part)
        groups = [[("tn", e, du)], [("tn", dy, hmid)]]
        grad = norm_step(l, 2, grad, de, n_2, r_2)

        dy = rows_of_all(grad.astype(LOW))
        dcq, dmkv, part = kernel_call(
            cross_backward,
            [*dy, cq, mkv, text_bias, clse, attn[l]],
            [low_frames, ((192, 2 * WIDE), LOW), partial_rows],
            specs=[None] * 6 + [cross_window[l]],
        )
        if l == 1:
            part, packs = tied(part, packs)
        dc = sum_to_rows(part)
        none = jnp.zeros_like(dmkv)
        dmkv = jnp.where(
            zh == 0, jnp.concatenate([dmkv, none]), jnp.concatenate([none, dmkv])
        )
        memory_terms.append(("nt", (attn[l], (384, 4 * l)), dmkv))
        cross = [[("nn", (piece_1, (384, 1)), dmkv)], [("tn", c, dcq), ("tn", dy, co)]]
        if l == 1:
            early = weight_sums(groups + cross, width)
            dc, early = tied(dc, early)
            early = summed(early)
        else:
            second = weight_sums(groups + late + cross + [memory_terms], width)
            dc, second, early = tied(dc, second, early)
            second = summed(second)
        grad = norm_step(l, 1, grad, dc, n_1, r_1)

        dy = rows_of_all(grad.astype(LOW))
        do_pack, delta = kernel_call(
            self_upstream,
            [*dy, o, attn[l]],
            [pack_rows, lse_rows],
            specs=[None] * 3 + [out_window[l]],
        )
        do_packs = keyed_of_all(do_pack)
        dq = kernel_call(
            self_query_grad,
            [qkv, *kv, bias, lse, do_pack, delta],
            [low_frames],
            room=32,
        )[0]
        dkv = kernel_call(
            self_key_grad,
            [keyed_order, qkv, back_bias, packs, *do_packs],
            [((frames, 2 * WIDE), LOW)],
            specs=[lambda x: pl.BlockSpec(memory_space=pltpu.SMEM), None, None, window(256, l)]
            + [None] * 8,
            room=32,
        )[0]
        dqkv = jnp.concatenate([dq, dkv], axis=1)
        da = nt(dqkv, w_in[l])
        late = [[("tn", a, dqkv), ("tn", dy, o)]]
        if l == 1:
            grad = norm_step(l, 0, grad, sum_to_rows(da), n_0, r_0)
        else:
            norm_terms[0, 0] = (da, unit_all)
            last = weight_sums(late, width)
            sums = kernel_call(
                norm_sums,
                [x for l, k in NORMS for x in norm_terms[l, k]],
                [((16, width), FULL)],
            )[0]
            extra = jnp.broadcast_to(sums[None], (8, *sums.shape))
            da = jnp.concatenate([da.reshape(8, -1, width), extra], axis=1)
            da = sum_to_rows(da.reshape(-1, width))
            da, last = tied(da, last)
            last = strip_of(sum_along(sum_along(strip_blocks(last), "y"), DEEP))
            norm_total = da[-16:].astype(LOW).reshape(16, 16, -1)
            norm_total = lax.all_to_all(jnp.swapaxes(norm_total, 0, 1), SPREAD, 0, 0, tiled=True)
            norm_total = jnp.sum(norm_total.astype(FULL), axis=0)
            grad = grad + unit_back(da[:-16], n_0, r_0, gains[0][0])
    ends = kernel_call(rows_restored, [residual, grad], [((32, 2 * width), LOW)])[0]
    ends = frames_back(ends)
    output, input_grad = ends[:, :, :width], ends[:, :, width:].astype(FULL)

    def strips(block):
        mine = lax.dynamic_slice_in_dim(block, xl * strip, strip, axis=0)
        theirs = lax.dynamic_slice_in_dim(block, (1 - xl) * strip, strip, axis=0)
        return mine, swapped(theirs, "xl")

    def both(pair, start, size):
        return sum(x[:, start : start + size].astype(FULL) for x in pair)

    def everywhere(x):
        x = x + swapped(x.astype(LOW), "core").astype(FULL)
        return x + swapped(x.astype(LOW), "xh").astype(FULL)

    early, second, last = [strips(b) for b in (early, second, last)]
    laid = laid_out((early, second, last), xl, strip, ff)
    self_in_grad, self_out_grad, text_query_grad, text_kv_grad = laid[:4]
    text_out_grad, mlp_up_grad, mlp_down_grad = laid[4:]
    self_out_grad, text_out_grad, mlp_down_grad = [
        jnp.swapaxes(x, 1, 2) for x in (self_out_grad, text_out_grad, mlp_down_grad)
    ]
    memory_grad = everywhere(both(second, 3072, 384)).reshape(strip, 2, 192)
    memory_grad = jnp.transpose(memory_grad, (1, 2, 0))
    norm_grads = lax.dynamic_slice_in_dim(norm_total, xl * strip, strip, axis=1)
    gain_grad = norm_grads[:6].reshape(2, 3, strip)
    shift_grad = norm_grads[6:12].reshape(2, 3, strip)
    return (
        output,
        input_grad,
        memory_grad,
        gain_grad,
        shift_grad[:, 0:2],
        shift_grad[:, 2],
        self_in_grad,
        self_out_grad,
        text_query_grad,
        text_kv_grad,
        text_out_grad,
        mlp_up_grad,
        mlp_down_grad,
    )


def solution(mesh):
    fine = Mesh(mesh.devices.reshape(FINE_SIZES), FINE)
    frames = P(None, COL, None)
    strips = P(None, None, COL)
    return jax.shard_map(
        local,
        mesh=fine,
        in_specs=(
            frames,
            strips,
            P(),
            frames,
            strips,
            strips,
            P(None, None, COL, ROW),
            P(None, ROW, COL),
            P(None, COL, ROW),
            P(None, None, COL, ROW),
            P(None, ROW, COL),
            P(None, COL, ROW),
            P(None, ROW, COL),
        ),
        out_specs=(
            frames,
            frames,
            strips,
            strips,
            strips,
            P(None, COL),
            P(None, None, COL, ROW),
            P(None, ROW, COL),
            P(None, COL, ROW),
            P(None, None, COL, ROW),
            P(None, ROW, COL),
            P(None, COL, ROW),
            P(None, ROW, COL),
        ),
        check_vma=False,
    )
```
